128 devices in a mesh: ep: 16 (over z_lo, y, core), fsdp: 8 (over x, z_hi).
Axes of the slice: x: 4, y: 4, z: 4 (z_hi: 2, z_lo: 2; z = z_hi * 2 + z_lo), core: 2. Of those that a mesh axis runs over, the one named last changes fastest.
Arguments:
- moe_input: bfloat16 [4608, 7168], P(('ep', 'fsdp')), may hold values from -6 to 6
- out_grad: bfloat16 [4608, 7168], P(('ep', 'fsdp')), may hold values from -6 to 6
- expert_ids: int32 [4608, 1], P(('ep', 'fsdp')), may hold values from 0 to 15; in each aligned block of 36 rows (0 to 35, 36 to 71, ...) at most 7 rows name the same one
- gate_values: bfloat16 [4608, 1], P(('ep', 'fsdp')), may hold values from 0.19921875 to 1
- w_gate: bfloat16 [16, 7168, 2048], P('ep', None, 'fsdp'), may hold values from -0.0625 to 0.0625
- w_up: bfloat16 [16, 7168, 2048], P('ep', None, 'fsdp'), may hold values from -0.0625 to 0.0625
- w_down: bfloat16 [16, 2048, 7168], P('ep', 'fsdp'), may hold values from -0.125 to 0.125
Outputs:
- moe_grad: bfloat16 [4608, 7168], P(('ep', 'fsdp'))
- gate_grad: bfloat16 [4608, 1], P(('ep', 'fsdp'))
- grad_w_gate: bfloat16 [16, 7168, 2048], P('ep', None, 'fsdp')
- grad_w_up: bfloat16 [16, 7168, 2048], P('ep', None, 'fsdp')
- grad_w_down: bfloat16 [16, 2048, 7168], P('ep', 'fsdp')
The draws below stay inside these ranges and needn't reach their ends.
Inputs may be any that keep to these rules, and one draw needn't show every extreme that they name: `expert_ids`: in each aligned block of 36 rows (the rows of one device) no expert is named by more than 7 routes, and in every draw some block names one expert exactly 7 times.
All inputs are finite; a program needn't handle non-finite values.
Results may differ from the reference program's by a relative error of at most 0.022.
Values may be sent and summed in bfloat16 or wider, within the bound.
A program may use at most 192 MiB of HBM per device.

```python
import math
import jax
import jax.numpy as jnp
import numpy as np
from jax import lax

D = 7168
FF = 2048
TOK_DEV = 36
TOPW = 1
EXPERTS = 16
TOKENS = 4608
CAP = 7
ROWS = 896
N_FSDP = 8


def steps_of(key, extent, cuts, smallest, largest):
    def one(position, parts):
        draws = jax.random.uniform(jax.random.fold_in(jax.random.fold_in(key, 6), position), (parts,), jnp.float32, smallest / len(cuts), largest / len(cuts))
        return jnp.repeat(jnp.exp(draws), extent[position] // parts).reshape((-1,) + (1,) * (len(extent) - position - 1))

    factor_of = one(*cuts[0])
    for cut in cuts[1:]:
        factor_of = factor_of * one(*cut)
    return factor_of


def routed_block(rng, own, number, rows, count, top, most, skew):
    ranking = jax.random.permutation(rng, count)
    heavy_load, common = load_shares(count, rows * top, most, skew, True), load_shares(count, rows * top, most, skew, False)
    places = jnp.arange(count)

    def named(sizes, turn):
        used = int((sizes > 0).sum())
        fixed = max(1, used // 4)
        passed = fixed + (places - fixed + turn * (used - fixed)) % max(1, count - fixed)
        return jnp.zeros((count,), jnp.int32).at[ranking[jnp.where(places < fixed, places, passed)]].set(jnp.asarray(sizes, jnp.int32))

    sizes = jnp.where(number % 4 == 0, named(heavy_load, number // 4), named(common, number - number // 4 - 1))
    mixed = jax.random.permutation(jax.random.fold_in(own, 3), count)
    donor, sink = mixed[0:count // 2 * 2:2], mixed[1:count // 2 * 2:2]
    room = jnp.minimum(sizes[donor] - 1, most - sizes[sink]) // 2
    room = jnp.where((donor == ranking[0]) | (sink == ranking[0]) | (sizes[sink] == 0), 0, jnp.maximum(room, 0))
    passed = jax.random.randint(jax.random.fold_in(own, 4), (count // 2,), 0, 1 << 20) % (room + 1)
    sizes = sizes.at[donor].add(-passed).at[sink].add(passed)
    labels = jnp.searchsorted(jnp.cumsum(sizes), jnp.arange(rows * top), side="right").astype(jnp.int32)
    listing = labels.reshape(top, rows).T
    listing = listing[jax.random.permutation(jax.random.fold_in(own, 1), rows)]
    turn = jax.random.randint(jax.random.fold_in(own, 2), (rows, 1), 0, top)
    return jnp.take_along_axis(listing, (jnp.arange(top)[None, :] + turn) % top, axis=1)


def load_shares(number_of, total, most, lean, full):
    weights = [(1 << 20) // math.isqrt(standing ** lean) + 1 for standing in range(1, number_of + 1)]
    largest = most if full else min(most, max(-(-total // number_of), total * weights[0] // sum(weights)))
    least = 1 if total - largest >= number_of - 1 else 0
    holding, surplus = [largest] + [least] * (number_of - 1), total - largest - least * (number_of - 1)
    while surplus > 0:
        movable = [i for i in range(1, number_of) if holding[i] < largest] or [i for i in range(1, number_of) if holding[i] < most]
        whole, remaining = sum([weights[i] for i in movable]), surplus
        for i in movable:
            more = min(most - holding[i], max(1, remaining * weights[i] // whole), surplus)
            holding[i] = holding[i] + more
            surplus = surplus - more
    return np.array(holding)


def noise(rng, dims, scale, bound, cuts=(), kind=jnp.bfloat16):
    result = jax.random.normal(rng, dims, jnp.float32) * scale
    if len(cuts) > 0:
        result = steps_of(rng, dims, cuts, -0.22, 0.18) * result
    return jnp.clip(result, min=-bound, max=bound).astype(kind)


def setup_inputs(seed: int = 0) -> dict:
    key_list = jax.random.split(jax.random.key(seed), 8)
    moe_input = noise(key_list[0], (TOKENS, D), 1.0, 6.0, ((0, 128),))
    out_grad = noise(key_list[1], (TOKENS, D), 1.0, 6.0, ((0, 128),))
    expert_ids_keys = jax.random.split(jax.random.fold_in(key_list[2], 1), TOKENS // TOK_DEV)
    expert_ids_turns = jax.random.permutation(jax.random.fold_in(key_list[2], 3), TOKENS // TOK_DEV)
    expert_ids = jax.vmap(lambda own, number: routed_block(jax.random.fold_in(key_list[2], 2), own, number, TOK_DEV, EXPERTS, TOPW, CAP, 2))(expert_ids_keys, expert_ids_turns).reshape((TOKENS, TOPW))
    gate_values = jnp.clip(0.19921875 + 0.80078125 * jax.random.uniform(key_list[3], (TOKENS, TOPW), jnp.float32) ** steps_of(key_list[3], (TOKENS, TOPW), ((0, 128),), -0.2, 0.2), 0.19921875, 1.0).astype(jnp.bfloat16)
    w_gate = noise(key_list[4], (EXPERTS, D, FF), D ** -0.5, 0.0625, ((0, 16), (2, 8)))
    w_up = noise(key_list[5], (EXPERTS, D, FF), D ** -0.5, 0.0625, ((0, 16), (2, 8)))
    w_down = noise(key_list[6], (EXPERTS, FF, D), FF ** -0.5, 0.125, ((0, 16), (1, 8)))
    return dict(moe_input=moe_input, out_grad=out_grad, expert_ids=expert_ids, gate_values=gate_values, w_gate=w_gate, w_up=w_up, w_down=w_down)


def silu_parts(value):
    sig = jax.nn.sigmoid(value)
    return (value * sig, sig * (1.0 + value * (1.0 - sig)))

def reference(moe_input, out_grad, expert_ids, gate_values, w_gate, w_up, w_down):
    routes = TOKENS * TOPW
    units = FF // N_FSDP
    flat_ids = expert_ids.reshape(routes).astype(jnp.int32)
    route_input = jnp.concatenate([jnp.repeat(moe_input, TOPW, axis=0), jnp.zeros((1, D), moe_input.dtype)], axis=0)
    route_grad = jnp.concatenate([jnp.repeat(out_grad, TOPW, axis=0), jnp.zeros((1, D), out_grad.dtype)], axis=0)
    route_gate = jnp.concatenate([gate_values.reshape(routes), jnp.zeros((1,), gate_values.dtype)], axis=0)
    expert_scale = 1.0 / math.sqrt(TOKENS // EXPERTS)
    gate_scale = 1.0 / math.sqrt(D)

    def one_expert(expert):
        chosen = jnp.nonzero(flat_ids == expert, size=ROWS, fill_value=routes)[0].astype(jnp.int32)
        rows_in = route_input[chosen]
        rows_grad = route_grad[chosen]
        gates = route_gate[chosen].astype(jnp.float32)[:, None]
        weight_gate = w_gate[expert]
        weight_up = w_up[expert]
        weight_down = w_down[expert]
        pre_gate = jnp.dot(rows_in, weight_gate, preferred_element_type=jnp.float32)
        pre_up = jnp.dot(rows_in, weight_up, preferred_element_type=jnp.float32)
        act, slope = silu_parts(pre_gate)
        hidden = (act * pre_up).astype(jnp.bfloat16)
        raw = jnp.dot(rows_grad, weight_down.T, preferred_element_type=jnp.float32)
        scaled = gates * raw
        grad_pre_gate = (scaled * pre_up * slope).astype(jnp.bfloat16)
        grad_pre_up = (scaled * act).astype(jnp.bfloat16)
        gated_grad = (gates * rows_grad.astype(jnp.float32)).astype(jnp.bfloat16)
        grad_gate = (jnp.dot(rows_in.T, grad_pre_gate, preferred_element_type=jnp.float32) * expert_scale).astype(jnp.bfloat16)
        grad_up = (jnp.dot(rows_in.T, grad_pre_up, preferred_element_type=jnp.float32) * expert_scale).astype(jnp.bfloat16)
        grad_down = (jnp.dot(hidden.T, gated_grad, preferred_element_type=jnp.float32) * expert_scale).astype(jnp.bfloat16)
        pieces = jnp.einsum('rkf,dkf->rkd', grad_pre_gate.astype(jnp.float32).reshape(ROWS, N_FSDP, units), weight_gate.astype(jnp.float32).reshape(D, N_FSDP, units))
        pieces = pieces + jnp.einsum('rkf,dkf->rkd', grad_pre_up.astype(jnp.float32).reshape(ROWS, N_FSDP, units), weight_up.astype(jnp.float32).reshape(D, N_FSDP, units))
        pieces = lax.optimization_barrier(pieces.astype(jnp.bfloat16)).astype(jnp.float32)
        route_row = lax.optimization_barrier(jnp.sum(pieces, axis=1)).astype(jnp.bfloat16)
        gate_piece = lax.optimization_barrier(jnp.sum((hidden.astype(jnp.float32) * raw).reshape(ROWS, N_FSDP, units), axis=2)) * gate_scale
        gate_piece = lax.optimization_barrier(gate_piece.astype(jnp.bfloat16)).astype(jnp.float32)
        route_gate_grad = lax.optimization_barrier(jnp.sum(gate_piece, axis=1)).astype(jnp.bfloat16)
        return (grad_gate, grad_up, grad_down, route_row, route_gate_grad, chosen)
    grad_w_gate, grad_w_up, grad_w_down, route_rows, route_gates, chosen = lax.map(one_expert, jnp.arange(EXPERTS, dtype=jnp.int32))
    flat_chosen = chosen.reshape(EXPERTS * ROWS).astype(jnp.int32)
    route_dx = jnp.zeros((routes + 1, D), jnp.bfloat16).at[flat_chosen].set(route_rows.reshape(EXPERTS * ROWS, D))[:routes]
    moe_grad = lax.optimization_barrier(jnp.sum(route_dx.astype(jnp.float32).reshape(TOKENS, TOPW, D), axis=1)).astype(jnp.bfloat16)
    gate_grad = jnp.zeros((routes + 1,), jnp.bfloat16).at[flat_chosen].set(route_gates.reshape(EXPERTS * ROWS))[:routes]
    gate_grad = gate_grad.reshape(TOKENS, TOPW)
    return (moe_grad, gate_grad, grad_w_gate, grad_w_up, grad_w_down)
```

```python
import functools
import math

import jax
import jax.numpy as jnp
from jax import lax
from jax.experimental import pallas as pl
from jax.experimental.pallas import tpu as pltpu
from jax.sharding import PartitionSpec as P

BF = jnp.bfloat16
F32 = jnp.float32
CAP = 7
UNIT = 16
STEPS = 4
BLOCKS = 8
HALF = BLOCKS * CAP
DENSE = 2 * HALF
CUT = 64
LANES = 128


def nn(left, right):
    return jnp.dot(left, right, preferred_element_type=F32)


def nt(left, right):
    return lax.dot_general(left, right, (((1,), (1,)), ((), ())), preferred_element_type=F32)


def kernel(
    units_hbm, w_gate_hbm, w_up_hbm, w_down_hbm, low_map, high_map, inv_gate,
    moe_grad, gate_grad, grad_gate_hbm, grad_up_hbm, grad_down_hbm, returned_hbm,
    w_gate, w_up, w_down, arrived, chunks, part, far_in, near_in, back, acc, packed, turned,
    w_sem, unit_send, unit_recv, own_send, own_recv, fwd_send, fwd_recv,
    far_send, far_recv, near_send, near_recv, far_free, near_free,
    back_send, back_recv, out_sem,
):
    width = w_gate.shape[0]
    units_of = w_gate.shape[1]
    half_width = width // 2
    ep = lax.axis_index("ep")
    fs = lax.axis_index("fsdp")
    z = lax.rem(fs, 2) * 2 + ep // 8
    y = lax.rem(ep // 2, 4)
    core = lax.rem(ep, 2)
    x = fs // 2

    def at(ax, ay, az, ac):
        return (lax.rem(az, 2) * 8 + ay * 2 + ac, ax * 2 + az // 2)

    def shift(v, n):
        return lax.rem(v + n, 4)

    plus = at(shift(x, 1), y, z, core)
    minus = at(shift(x, 3), y, z, core)
    remote = functools.partial(
        pltpu.make_async_remote_copy, device_id_type=pl.DeviceIdType.MESH
    )

    partners = [plus, minus]
    for dy in range(4):
        for dz in range(4):
            for dc in range(2):
                if dy or dz or dc:
                    partners.append(at(x, shift(y, dy), shift(z, dz), lax.rem(core + dc, 2)))

    weights = [
        pltpu.make_async_copy(w_gate_hbm.at[0], w_gate, w_sem.at[0]),
        pltpu.make_async_copy(w_up_hbm.at[0], w_up, w_sem.at[1]),
        pltpu.make_async_copy(w_down_hbm.at[0], w_down, w_sem.at[2]),
    ]

    barrier = pltpu.get_barrier_semaphore()
    for partner in partners:
        pl.semaphore_signal(barrier, 1, device_id=partner, device_id_type=pl.DeviceIdType.MESH)
    pl.semaphore_wait(barrier, len(partners))

    mine = z * 2 + core
    unit_copies = []
    for k in range(STEPS):
        for dz in range(4):
            for dc in range(2):
                ay, az, ac = shift(y, 4 - k), shift(z, dz), lax.rem(core + dc, 2)
                expert = lax.rem(az, 2) * 8 + ay * 2 + ac
                src = units_hbm.at[expert]
                dst = arrived.at[k * BLOCKS + mine]
                index = (k * 4 + dz) * 2 + dc
                sem = unit_recv.at[k * BLOCKS + mine]
                if k or dz or dc:
                    copy = remote(src, dst, unit_send.at[index], sem, device_id=at(x, ay, az, ac))
                    copy.start()
                    unit_copies.append(copy)
                else:
                    pltpu.make_async_copy(src, dst, sem).start()
    for copy in weights:
        copy.start()

    row = lax.broadcasted_iota(jnp.int32, (DENSE, BLOCKS * UNIT), 0)
    col = lax.broadcasted_iota(jnp.int32, (DENSE, BLOCKS * UNIT), 1)
    upper = (row >= HALF).astype(jnp.int32)
    rest = row - upper * HALF
    block = jnp.zeros_like(row)
    for b in range(1, BLOCKS):
        block = block + (rest >= CAP * b).astype(jnp.int32)
    place = block * UNIT + upper * CAP + (rest - block * CAP)
    select = (col == place).astype(F32).astype(BF)
    row_t = lax.broadcasted_iota(jnp.int32, (BLOCKS * UNIT, DENSE), 1)
    col_t = lax.broadcasted_iota(jnp.int32, (BLOCKS * UNIT, DENSE), 0)
    upper_t = (row_t >= HALF).astype(jnp.int32)
    rest_t = row_t - upper_t * HALF
    block_t = jnp.zeros_like(row_t)
    for b in range(1, BLOCKS):
        block_t = block_t + (rest_t >= CAP * b).astype(jnp.int32)
    place_t = block_t * UNIT + upper_t * CAP + (rest_t - block_t * CAP)
    select_t = (col_t == place_t).astype(F32).astype(BF)

    own = {}
    fwd = {}
    far = {}
    near = {}
    backs = {}

    def take_in(k):
        for b in range(BLOCKS):
            j = k * BLOCKS + b
            pltpu.make_async_copy(arrived.at[j], arrived.at[j], unit_recv.at[j]).wait()
        step = 1024

        def move(i, carry):
            cols = pl.ds(pl.multiple_of(i * step, step), step)
            found = arrived[k * BLOCKS : (k + 1) * BLOCKS, :, cols].reshape(BLOCKS * UNIT, step)
            chunks[k, 0, :, cols] = nn(select, found).astype(BF)
            return carry

        lax.fori_loop(0, width // step, move, 0)
        own[k] = [
            remote(chunks.at[k, 0], chunks.at[k, 1], own_send.at[k, 0], own_recv.at[k, 0], device_id=plus),
            remote(chunks.at[k, 0], chunks.at[k, 2], own_send.at[k, 1], own_recv.at[k, 1], device_id=minus),
        ]
        for copy in own[k]:
            copy.start()

    def forward(k):
        low, high = pl.ds(0, CUT), pl.ds(CUT, DENSE - CUT)
        fwd[k] = [
            remote(chunks.at[k, 1, low], chunks.at[k, 3, low], fwd_send.at[k, 0], fwd_recv.at[k, 0], device_id=plus),
            remote(chunks.at[k, 2, high], chunks.at[k, 3, high], fwd_send.at[k, 1], fwd_recv.at[k, 1], device_id=minus),
        ]
        for i in range(2):
            own[k][i].wait_recv()
            fwd[k][i].start()

    def compute(k):
        for copy in fwd[k]:
            copy.wait_recv()
        rows = 4 * DENSE
        step = 1024
        acc[...] = jnp.zeros_like(acc)

        def gather(i, carry):
            cols = pl.ds(pl.multiple_of(i * step, step), step)
            left = chunks[k, :, :, cols].reshape(rows, step)
            acc[0:rows, 0:units_of] += nn(left, w_gate[cols, :])
            acc[0:rows, units_of : 2 * units_of] += nn(left, w_up[cols, :])
            acc[0:rows, 2 * units_of : 3 * units_of] += nt(left, w_down[:, cols])
            return carry

        lax.fori_loop(0, width // step, gather, 0)
        if k:
            for copy in far[k - 1] + near[k - 1]:
                copy.wait_send()
        blank = jnp.zeros((HALF, units_of), F32)
        for r in range(4):
            ins = pl.ds(r * DENSE, HALF)
            outs = pl.ds(r * DENSE + HALF, HALF)
            pre_gate = acc[ins, 0:units_of]
            pre_up = acc[ins, units_of : 2 * units_of]
            scaled = acc[outs, 2 * units_of : 3 * units_of]
            sig = jax.nn.sigmoid(pre_gate)
            act = pre_gate * sig
            slope = sig * (1.0 + pre_gate * (1.0 - sig))
            hidden = (act * pre_up).astype(BF).astype(F32)
            grad_gate = scaled * pre_up * slope
            grad_up = scaled * act
            piece = jnp.sum(hidden * scaled, axis=1, keepdims=True) * (1.0 / math.sqrt(width))
            acc[ins, 0:units_of] = grad_gate
            acc[ins, units_of : 2 * units_of] = grad_up
            acc[ins, 2 * units_of : 3 * units_of] = blank
            acc[outs, 0:units_of] = blank
            acc[outs, units_of : 2 * units_of] = blank
            acc[outs, 2 * units_of : 3 * units_of] = hidden
            packed[r * HALF : (r + 1) * HALF, 0:units_of] = grad_gate
            packed[r * HALF : (r + 1) * HALF, units_of : 2 * units_of] = grad_up
            part[r, :, half_width : half_width + LANES] = jnp.concatenate(
                [jnp.broadcast_to(piece, (HALF, LANES)), jnp.zeros((HALF, LANES), F32)], axis=0
            ).astype(BF)
        turned[k] = jnp.transpose(acc[...]).astype(BF)
        left_gate = packed[:, 0:units_of].astype(BF)
        left_up = packed[:, units_of : 2 * units_of].astype(BF)
        span = 512

        def rows_back(i, carry):
            lo = pl.ds(pl.multiple_of(i * span, span), span)
            hi = pl.ds(pl.multiple_of(half_width + i * span, span), span)
            r_lo = nt(left_gate, w_gate[lo, :]) + nt(left_up, w_up[lo, :])
            r_hi = nt(left_gate, w_gate[hi, :]) + nt(left_up, w_up[hi, :])
            for r in range(4):
                mine_rows = slice(r * HALF, (r + 1) * HALF)
                part[r, :, lo] = jnp.concatenate([r_lo[mine_rows], r_hi[mine_rows]], axis=0).astype(BF)
            return carry

        lax.fori_loop(0, half_width // span, rows_back, 0)
        if k:
            pl.semaphore_wait(far_free, 2)
        low, high = pl.ds(0, CUT), pl.ds(CUT, DENSE - CUT)
        far[k] = [
            remote(part.at[3, low], far_in.at[0, low], far_send.at[k, 0], far_recv.at[k, 0], device_id=plus),
            remote(part.at[3, high], far_in.at[1, high], far_send.at[k, 1], far_recv.at[k, 1], device_id=minus),
        ]
        for copy in far[k]:
            copy.start()

    def pass_on(k):
        if k:
            pl.semaphore_wait(near_free, 2)
        near[k] = [
            remote(part.at[2], near_in.at[0], near_send.at[k, 0], near_recv.at[k, 0], device_id=plus),
            remote(part.at[1], near_in.at[1], near_send.at[k, 1], near_recv.at[k, 1], device_id=minus),
        ]
        for i, rel, rows, giver in ((0, 2, slice(0, CUT), minus), (1, 1, slice(CUT, DENSE), plus)):
            far[k][i].wait_recv()
            part[rel, rows] = (part[rel, rows].astype(F32) + far_in[i, rows].astype(F32)).astype(BF)
            if k < STEPS - 1:
                pl.semaphore_signal(far_free, 1, device_id=giver, device_id_type=pl.DeviceIdType.MESH)
            near[k][i].start()

    def send_back(k):
        for copy in near[k]:
            copy.wait_recv()
        slot = k % 2
        if k >= 2:
            for copy in backs[k - 2]:
                copy.wait_send()
        full = half_width + LANES
        for first in range(0, full, 1024):
            cols = slice(first, min(first + 1024, full))
            total = nn(select_t, part[0, :, cols]) + nn(select_t, near_in[0, :, cols])
            total = total + nn(select_t, near_in[1, :, cols])
            back[slot, :, :, cols] = total.astype(BF).reshape(BLOCKS, UNIT, cols.stop - cols.start)
        if k < STEPS - 1:
            for giver in (minus, plus):
                pl.semaphore_signal(near_free, 1, device_id=giver, device_id_type=pl.DeviceIdType.MESH)
        me = y * BLOCKS + mine
        backs[k] = []
        for dz in range(4):
            for dc in range(2):
                ay, az, ac = shift(y, k), shift(z, dz), lax.rem(core + dc, 2)
                src = back.at[slot, az * 2 + ac]
                index = (k * 4 + dz) * 2 + dc
                if k or dz or dc:
                    copy = remote(src, returned_hbm.at[me], back_send.at[index], back_recv.at[me], device_id=at(x, ay, az, ac))
                    copy.start()
                    backs[k].append(copy)
                else:
                    kept = pltpu.make_async_copy(src, returned_hbm.at[me], w_sem.at[1])
                    kept.start()
                    kept.wait()

    scale = 1.0 / math.sqrt(36 * 8)
    span = 512
    out_copies = []

    def gradients(first, last):
        def one(i, carry):
            cols = pl.ds(pl.multiple_of(i * span, span), span)
            total = nn(turned[0][:, 0 : 4 * DENSE], chunks[0, :, :, cols].reshape(4 * DENSE, span))
            for k in range(1, STEPS):
                total = total + nn(turned[k][:, 0 : 4 * DENSE], chunks[k, :, :, cols].reshape(4 * DENSE, span))
            total = total * scale
            w_gate[cols, :] = jnp.transpose(total[0:units_of]).astype(BF)
            w_up[cols, :] = jnp.transpose(total[units_of : 2 * units_of]).astype(BF)
            w_down[:, cols] = total[2 * units_of :].astype(BF)
            return carry

        lax.fori_loop(first, last, one, 0)
        rows = pl.ds(first * span, (last - first) * span)
        n = len(out_copies)
        made = [
            pltpu.make_async_copy(w_gate.at[rows], grad_gate_hbm.at[0, rows], out_sem.at[n]),
            pltpu.make_async_copy(w_up.at[rows], grad_up_hbm.at[0, rows], out_sem.at[n + 1]),
            pltpu.make_async_copy(w_down.at[:, rows], grad_down_hbm.at[0, :, rows], out_sem.at[n + 2]),
        ]
        for copy in made:
            copy.start()
        out_copies.extend(made)

    take_in(0)
    take_in(1)
    forward(0)
    take_in(2)
    forward(1)
    take_in(3)
    for copy in weights:
        copy.wait()
    compute(0)
    forward(2)
    pass_on(0)
    send_back(0)
    compute(1)
    forward(3)
    pass_on(1)
    send_back(1)
    compute(2)
    pass_on(2)
    send_back(2)
    compute(3)
    gradients(0, 4)
    pass_on(3)
    gradients(4, 9)
    send_back(3)
    gradients(9, 14)

    for k in range(STEPS):
        for dz in range(4):
            for dc in range(2):
                if k or dz or dc:
                    j = shift(y, 4 - k) * BLOCKS + shift(z, dz) * 2 + lax.rem(core + dc, 2)
                    pltpu.make_async_copy(back.at[0, 0], returned_hbm.at[j], back_recv.at[j]).wait()
    full = half_width + LANES
    pull = pltpu.make_async_copy(returned_hbm, arrived.at[:, :, pl.ds(0, full)], w_sem.at[0])
    pull.start()
    pull.wait()
    for first in range(0, half_width, 512):
        found = arrived[:, :, first : first + 512].reshape(STEPS * BLOCKS * UNIT, 512)
        moe_grad[:, first : first + 512] = nn(low_map[...], found).astype(BF)
        moe_grad[:, half_width + first : half_width + first + 512] = nn(high_map[...], found).astype(BF)
    found = arrived[:, :, half_width:full].reshape(STEPS * BLOCKS * UNIT, LANES)
    gate_grad[...] = (nn(low_map[...], found) * inv_gate[...]).astype(BF)

    for copy in out_copies:
        copy.wait()
    for copy in unit_copies:
        copy.wait_send()
    for k in range(STEPS):
        for copy in own[k] + fwd[k]:
            copy.wait_send()
    for copy in far[STEPS - 1] + near[STEPS - 1] + backs[STEPS - 2] + backs[STEPS - 1]:
        copy.wait_send()


def body(moe_input, out_grad, expert_ids, gate_values, w_gate, w_up, w_down):
    tok_rows, width = moe_input.shape
    hidden = w_gate.shape[2]
    experts = lax.axis_size("ep")
    ids = expert_ids.reshape(tok_rows)
    one_hot = (ids[:, None] == jnp.arange(experts, dtype=jnp.int32)[None, :]).astype(jnp.int32)
    same = (ids[:, None] == ids[None, :]).astype(jnp.int32)
    before = jnp.tril(jnp.ones((tok_rows, tok_rows), jnp.int32), -1)
    slot = jnp.sum(same * before, axis=1)
    gates = gate_values.reshape(tok_rows, 1).astype(F32)
    gated = (gates * out_grad.astype(F32)).astype(BF)
    target = ids * UNIT + slot
    unit_rows = jnp.arange(experts * UNIT, dtype=jnp.int32)[:, None]
    place_x = (unit_rows == target[None, :]).astype(BF)
    place_g = (unit_rows == target[None, :] + CAP).astype(BF)
    units = nn(
        jnp.concatenate([place_x, place_g], axis=1), jnp.concatenate([moe_input, gated], axis=0)
    ).astype(BF).reshape(experts, UNIT, width)
    place = jnp.arange(STEPS * BLOCKS * UNIT, dtype=jnp.int32)
    giver, giver_row = place // UNIT, place % UNIT
    giver_expert = ((giver // 2) % 2) * 8 + (giver // 8) * 2 + giver % 2
    from_expert = giver_expert[None, :] == ids[:, None]
    low_map = (from_expert & (giver_row[None, :] == slot[:, None])).astype(BF)
    high_map = (from_expert & (giver_row[None, :] == slot[:, None] + CAP)).astype(BF)
    inv_gate = jnp.broadcast_to(1.0 / gates, (tok_rows, LANES))
    full = width // 2 + LANES

    vmem = pl.BlockSpec(memory_space=pltpu.VMEM)
    anywhere = pl.BlockSpec(memory_space=pl.ANY)
    dma = pltpu.SemaphoreType.DMA
    grads = pl.pallas_call(
        kernel,
        out_shape=[
            jax.ShapeDtypeStruct((tok_rows, width), BF),
            jax.ShapeDtypeStruct((tok_rows, LANES), BF),
            jax.ShapeDtypeStruct(w_gate.shape, BF),
            jax.ShapeDtypeStruct(w_up.shape, BF),
            jax.ShapeDtypeStruct(w_down.shape, BF),
            jax.ShapeDtypeStruct((STEPS * BLOCKS, UNIT, full), BF),
        ],
        in_specs=[anywhere] * 4 + [vmem] * 3,
        out_specs=[vmem] * 2 + [anywhere] * 4,
        scratch_shapes=[
            pltpu.VMEM((width, hidden), BF),
            pltpu.VMEM((width, hidden), BF),
            pltpu.VMEM((hidden, width), BF),
            pltpu.VMEM((STEPS * BLOCKS, UNIT, width), BF),
            pltpu.VMEM((STEPS, 4, DENSE, width), BF),
            pltpu.VMEM((4, DENSE, full), BF),
            pltpu.VMEM((2, DENSE, full), BF),
            pltpu.VMEM((2, DENSE, full), BF),
            pltpu.VMEM((2, BLOCKS, UNIT, full), BF),
            pltpu.VMEM((512, 3 * hidden), F32),
            pltpu.VMEM((4 * HALF, 2 * hidden), F32),
            pltpu.VMEM((STEPS, 3 * hidden, 512), BF),
            dma((3,)),
            dma((32,)),
            dma((32,)),
            dma((STEPS, 2)),
            dma((STEPS, 2)),
            dma((STEPS, 2)),
            dma((STEPS, 2)),
            dma((STEPS, 2)),
            dma((STEPS, 2)),
            dma((STEPS, 2)),
            dma((STEPS, 2)),
            pltpu.SemaphoreType.REGULAR,
            pltpu.SemaphoreType.REGULAR,
            dma((32,)),
            dma((32,)),
            dma((9,)),
        ],
        compiler_params=pltpu.CompilerParams(
            collective_id=0, has_side_effects=True, vmem_limit_bytes=63 * 2**20
        ),
    )(units, w_gate, w_up, w_down, low_map, high_map, inv_gate)
    moe_grad, gate_wide, grad_gate, grad_up, grad_down, _ = grads
    return (moe_grad, gate_wide[:, 0:1], grad_gate, grad_up, grad_down)


def solution(mesh):
    rows = P(("ep", "fsdp"), None)
    columns = P("ep", None, "fsdp")
    return jax.shard_map(
        body,
        mesh=mesh,
        in_specs=(rows, rows, rows, rows, columns, columns, P("ep", "fsdp", None)),
        out_specs=(rows, rows, columns, columns, P("ep", "fsdp", None)),
        check_vma=False,
    )
```

```python
import functools
import math

import jax
import jax.numpy as jnp
from jax import lax
from jax.experimental import pallas as pl
from jax.experimental.pallas import tpu as pltpu
from jax.sharding import PartitionSpec as P

BF = jnp.bfloat16
F32 = jnp.float32
CAP = 7
UNIT = 16
FLAG_ROW = 2 * CAP
STEPS = 4
BLOCKS = 8
SLOTS = BLOCKS * UNIT
LIST = 80
ROWS = 4 * LIST
PADDED = 384
LANES = 128
MESH = pl.DeviceIdType.MESH


def nn(left, right):
    return jnp.dot(left, right, preferred_element_type=F32)


def nt(left, right):
    return lax.dot_general(left, right, (((1,), (1,)), ((), ())), preferred_element_type=F32)


def tn(left, right):
    return lax.dot_general(left, right, (((0,), (0,)), ((), ())), preferred_element_type=F32)


def iota(shape, dim):
    return lax.broadcasted_iota(jnp.int32, shape, dim)


def ones(where):
    return where.astype(F32).astype(BF)


def kernel(
    moe_input, out_grad, ids_col, ids_row, gates, w_gate_hbm, w_up_hbm, w_down_hbm,
    moe_grad, gate_grad, overflow, grad_gate_hbm, grad_up_hbm, grad_down_hbm, lists_hbm, returned_hbm,
    w_gate, w_up, w_down, units, arrived, dense, lists, picks, part, twin_out, twin_in, far_in, near_in, back,
    acc, packed, turned, flag_out, flag_in,
    w_sem, unit_send, unit_recv, own_send, own_recv, fwd_send, fwd_recv, twin_send, twin_recv,
    part_send, part_recv, far_send, far_recv, near_send, near_recv, part_free, far_free, near_free,
    back_send, back_recv, flag_send, flag_recv, pull_sem, out_sem,
):
    tokens, width = moe_input.shape
    hid = w_gate.shape[1]
    half = width // 2
    full = half + LANES
    ep = lax.axis_index("ep")
    fs = lax.axis_index("fsdp")
    z = lax.rem(fs, 2) * 2 + ep // 8
    y = lax.rem(ep // 2, 4)
    core = lax.rem(ep, 2)
    x = fs // 2
    mine = z * 2 + core
    other = 1 - core

    def at(ax, ay, az, ac):
        return (lax.rem(az, 2) * 8 + ay * 2 + ac, ax * 2 + az // 2)

    def shift(v, n):
        return lax.rem(v + n, 4)

    plus = at(shift(x, 1), y, z, core)
    minus = at(shift(x, 3), y, z, core)
    twin = at(x, y, z, other)
    remote = functools.partial(pltpu.make_async_remote_copy, device_id_type=MESH)
    offsets = [(dy, dz, dc) for dy in range(4) for dz in range(4) for dc in range(2)]

    def plane(dy, dz, dc):
        return shift(y, dy), shift(z, dz), lax.rem(core + dc, 2)

    weights = [
        pltpu.make_async_copy(w_gate_hbm.at[0], w_gate, w_sem.at[0]),
        pltpu.make_async_copy(w_up_hbm.at[0], w_up, w_sem.at[1]),
        pltpu.make_async_copy(w_down_hbm.at[0], w_down, w_sem.at[2]),
    ]
    barrier = pltpu.get_barrier_semaphore()
    partners = [plus, minus] + [at(x, *plane(*o)) for o in offsets[1:]]
    for partner in partners:
        pl.semaphore_signal(barrier, 1, device_id=partner, device_id_type=MESH)

    col_id, row_id = ids_col[...], ids_row[...]
    same = col_id == row_id
    above = iota((tokens, tokens), 0) < iota((tokens, tokens), 1)
    below = iota((tokens, tokens), 0) > iota((tokens, tokens), 1)
    slot_row = jnp.sum((same & above).astype(F32), axis=0, keepdims=True).astype(jnp.int32)
    slot_col = jnp.sum((same & below).astype(F32), axis=1, keepdims=True).astype(jnp.int32)
    target = (row_id // 2) * UNIT + (row_id % 2) * CAP + slot_row
    place = (iota((SLOTS, tokens), 0) == target).astype(F32)
    taken = jnp.sum(place, axis=1, keepdims=True)
    place = place.astype(BF)
    square = (SLOTS, SLOTS)
    spread = ones(iota(square, 1) == mine * UNIT + iota(square, 0) % UNIT)
    to_flag = ones(
        (iota(square, 0) % UNIT == FLAG_ROW) & (iota(square, 0) // UNIT == iota(square, 1) // UNIT)
    )
    flags = nn(to_flag, (taken * spread.astype(F32)).astype(BF))
    gate = gates[...].astype(F32)
    step = 1024

    def pack(i, carry):
        cols = pl.ds(pl.multiple_of(i * step, step), step)
        gated = (gate * out_grad[:, cols].astype(F32)).astype(BF)
        units[0, :, :, cols] = nn(place, moe_input[:, cols]).astype(BF).reshape(8, UNIT, step)
        units[1, :, :, cols] = nn(place, gated).astype(BF).reshape(8, UNIT, step)
        return carry

    lax.fori_loop(0, width // step, pack, 0)
    for a in range(2):
        head = units[a, :, :, 0:LANES].reshape(SLOTS, LANES).astype(F32)
        units[a, :, :, 0:LANES] = (head + flags).astype(BF).reshape(8, UNIT, LANES)
    from_pair = iota((tokens, 2 * SLOTS), 1)
    token_map = ones(
        (from_pair // 64 == (col_id // 2) % 4)
        & ((from_pair // UNIT) % 2 == col_id // 8)
        & (from_pair % UNIT == (col_id % 2) * CAP + slot_col)
    )
    pl.semaphore_wait(barrier, len(partners))

    unit_copies = []

    def units_out(k):
        for dz in range(4):
            for dc in range(2):
                ay, az, ac = plane((4 - k) % 4, dz, dc)
                src = units.at[ac, lax.rem(az, 2) * 4 + ay]
                dst = arrived.at[k * BLOCKS + mine]
                index = (k * 4 + dz) * 2 + dc
                sem = unit_recv.at[k * BLOCKS + mine]
                if k or dz or dc:
                    copy = remote(src, dst, unit_send.at[index], sem, device_id=at(x, ay, az, ac))
                    copy.start()
                    unit_copies.append(copy)
                else:
                    pltpu.make_async_copy(src, dst, sem).start()

    earlier = ones(iota(square, 0) < iota(square, 1))
    owner = iota(square, 0) % UNIT
    lane = iota(square, 1)
    whose = ones(((lane == 0) & (owner < CAP)) | ((lane == 1) & (owner >= CAP) & (owner < 2 * CAP)))
    own, kept, fwd, twins, parts, far, near, backs = ({} for _ in range(8))
    over = [jnp.zeros((1, 1), F32)]

    def take_in(k):
        for b in range(BLOCKS):
            j = k * BLOCKS + b
            pltpu.make_async_copy(arrived.at[j], arrived.at[j], unit_recv.at[j]).wait()
        tiles = arrived[k * BLOCKS : (k + 1) * BLOCKS, :, 0:LANES].astype(F32)
        flag = jnp.where(iota(tiles.shape, 1) == FLAG_ROW, tiles, 0.0)
        flag = jnp.sum(flag.reshape(SLOTS, LANES), axis=0, keepdims=True)
        rank = nn(flag.astype(BF), earlier)
        count = jnp.sum(flag, axis=1, keepdims=True)
        over[0] = jnp.maximum(over[0], (count > LIST).astype(F32))
        pick = ones((iota((LIST, SLOTS), 0).astype(F32) == rank) & (flag > 0.5))
        picks[k] = pick
        masks = nn(pick, whose) + jnp.where(iota((LIST, LANES), 1) == 2, over[0], 0.0)
        dense[k, :, width : width + LANES] = masks.astype(BF)

        def move(i, carry):
            cols = pl.ds(pl.multiple_of(i * step, step), step)
            found = arrived[k * BLOCKS : (k + 1) * BLOCKS, :, cols].reshape(SLOTS, step)
            dense[k, :, cols] = nn(pick, found).astype(BF)
            return carry

        lax.fori_loop(0, width // step, move, 0)
        to = lists_hbm.at[core, k]
        own[k] = [
            remote(dense.at[k], to.at[1], own_send.at[k, 0], own_recv.at[k, 0], device_id=plus),
            remote(dense.at[k], to.at[2], own_send.at[k, 1], own_recv.at[k, 1], device_id=minus),
        ]
        twins[k] = [remote(dense.at[k], to.at[0], twin_send.at[k, 0], twin_recv.at[k, 0], device_id=twin)]
        kept[k] = pltpu.make_async_copy(dense.at[k], to.at[0], own_send.at[k, 2])
        for copy in own[k] + twins[k] + [kept[k]]:
            copy.start()

    def forward(k):
        to = lists_hbm.at[core, k]
        cut = 48 if k % 2 == 0 else 32
        low, high = pl.ds(0, cut), pl.ds(cut, LIST - cut)
        fwd[k] = [
            remote(to.at[1, low], to.at[3, low], fwd_send.at[k, 0], fwd_recv.at[k, 0], device_id=plus),
            remote(to.at[2, high], to.at[3, high], fwd_send.at[k, 1], fwd_recv.at[k, 1], device_id=minus),
        ]
        for i in range(2):
            own[k][i].wait_recv()
            fwd[k][i].start()
            copy = remote(to.at[i + 1], to.at[i + 1], twin_send.at[k, i + 1], twin_recv.at[k, i + 1], device_id=twin)
            copy.start()
            twins[k].append(copy)

    def share(k):
        to = lists_hbm.at[core, k]
        for copy in fwd[k]:
            copy.wait_recv()
        copy = remote(to.at[3], to.at[3], twin_send.at[k, 3], twin_recv.at[k, 3], device_id=twin)
        copy.start()
        twins[k].append(copy)

    def compute(k):
        kept[k].wait()
        for copy in twins[k]:
            copy.wait_recv()
        pull = pltpu.make_async_copy(lists_hbm.at[:, k], lists, pull_sem.at[0])
        pull.start()
        acc[...] = jnp.zeros_like(acc)
        pull.wait()

        def gather(i, carry):
            cols = pl.ds(pl.multiple_of(i * step, step), step)
            left = lists[0, :, :, cols].reshape(ROWS, step)
            acc[0:ROWS, 0:hid] += nn(left, w_gate[cols, :])
            acc[0:ROWS, hid : 2 * hid] += nn(left, w_up[cols, :])
            acc[0:ROWS, 2 * hid : 3 * hid] += nt(lists[1, :, :, cols].reshape(ROWS, step), w_down[:, cols])
            return carry

        lax.fori_loop(0, width // step, gather, 0)
        if k:
            for copy in [parts[k - 1]] + far[k - 1] + near[k - 1]:
                copy.wait_send()
        for r in range(4):
            rows = slice(r * LIST, (r + 1) * LIST)
            tile = lists[0, r, :, width : width + LANES].astype(F32)
            mask = jnp.sum(jnp.where(iota(tile.shape, 1) == core, tile, 0.0), axis=1, keepdims=True)
            pre_gate = acc[rows, 0:hid]
            pre_up = acc[rows, hid : 2 * hid]
            scaled = acc[rows, 2 * hid : 3 * hid] * mask
            sig = jax.nn.sigmoid(pre_gate)
            act = pre_gate * sig
            slope = sig * (1.0 + pre_gate * (1.0 - sig))
            hidden = (act * pre_up).astype(BF).astype(F32) * mask
            piece = jnp.sum(hidden * scaled, axis=1, keepdims=True) * (1.0 / math.sqrt(width))
            acc[rows, 0:hid] = scaled * pre_up * slope
            acc[rows, hid : 2 * hid] = scaled * act
            acc[rows, 2 * hid : 3 * hid] = hidden
            wide = jnp.broadcast_to(piece, (LIST, LANES)).astype(BF)
            part[r, :, half:full] = wide
            twin_out[r, :, half:full] = wide
        turned[k] = jnp.transpose(acc[...]).astype(BF)
        packed[...] = acc[0:ROWS, 0 : 2 * hid].astype(BF)
        span = 512

        def rows_back(into, first):
            def one(i, carry):
                cols = pl.ds(pl.multiple_of(i * span, span), span)
                here = pl.ds(pl.multiple_of(first + i * span, span), span)
                total = nt(packed[:, 0:hid], w_gate[here, :]) + nt(packed[:, hid : 2 * hid], w_up[here, :])
                into[:, :, cols] = total.astype(BF).reshape(4, LIST, span)
                return carry

            lax.fori_loop(0, half // span, one, 0)

        rows_back(twin_out, other * half)
        if k:
            pl.semaphore_wait(part_free, 1)
        parts[k] = remote(twin_out, twin_in, part_send.at[k], part_recv.at[k], device_id=twin)
        parts[k].start()
        rows_back(part, core * half)

    def merge(k):
        parts[k].wait_recv()

        def add(r, carry):
            part[r] = (part[r].astype(F32) + twin_in[r].astype(F32)).astype(BF)
            return carry

        cut = 48 if k % 2 == 0 else 32
        low, high = pl.ds(0, cut), pl.ds(cut, LIST - cut)
        part[3] = (part[3].astype(F32) + twin_in[3].astype(F32)).astype(BF)
        if k:
            pl.semaphore_wait(far_free, 2)
        far[k] = [
            remote(part.at[3, low], far_in.at[0, low], far_send.at[k, 0], far_recv.at[k, 0], device_id=plus),
            remote(part.at[3, high], far_in.at[1, high], far_send.at[k, 1], far_recv.at[k, 1], device_id=minus),
        ]
        for copy in far[k]:
            copy.start()
        lax.fori_loop(0, 3, add, 0)
        if k < STEPS - 1:
            pl.semaphore_signal(part_free, 1, device_id=twin, device_id_type=MESH)

    def pass_on(k):
        if k:
            pl.semaphore_wait(near_free, 2)
        near[k] = [
            remote(part.at[2], near_in.at[0], near_send.at[k, 0], near_recv.at[k, 0], device_id=plus),
            remote(part.at[1], near_in.at[1], near_send.at[k, 1], near_recv.at[k, 1], device_id=minus),
        ]
        cut = 48 if k % 2 == 0 else 32
        for i, rel, rows, giver in ((0, 2, slice(0, cut), minus), (1, 1, slice(cut, LIST), plus)):
            far[k][i].wait_recv()
            part[rel, rows] = (part[rel, rows].astype(F32) + far_in[i, rows].astype(F32)).astype(BF)
            if k < STEPS - 1:
                pl.semaphore_signal(far_free, 1, device_id=giver, device_id_type=MESH)
            near[k][i].start()

    def send_back(k):
        for copy in near[k]:
            copy.wait_recv()
        slot = k % 2
        if k >= 2:
            for copy in backs[k - 2]:
                copy.wait_send()
        for first in range(0, full, 1024):
            cols = slice(first, min(first + 1024, full))
            total = tn(picks[k], part[0, :, cols]) + tn(picks[k], near_in[0, :, cols])
            total = total + tn(picks[k], near_in[1, :, cols])
            back[slot, :, :, cols] = total.astype(BF).reshape(BLOCKS, UNIT, cols.stop - cols.start)
        if k < STEPS - 1:
            for giver in (minus, plus):
                pl.semaphore_signal(near_free, 1, device_id=giver, device_id_type=MESH)
        me = core * 16 + y * 4 + z
        backs[k] = []
        for dz in range(4):
            for dc in range(2):
                ay, az, ac = plane(k, dz, dc)
                src = back.at[slot, az * 2 + ac]
                index = (k * 4 + dz) * 2 + dc
                if k or dz or dc:
                    copy = remote(src, returned_hbm.at[me], back_send.at[index], back_recv.at[me], device_id=at(x, ay, az, ac))
                    copy.start()
                    backs[k].append(copy)
                else:
                    stay = pltpu.make_async_copy(src, returned_hbm.at[me], pull_sem.at[1])
                    stay.start()
                    stay.wait()

    flag_copies = []

    def tell():
        tile = jnp.maximum(lists[0, 0, 0:16, width : width + LANES], lists[0, 1, 0:16, width : width + LANES])
        tile = jnp.maximum(tile, lists[0, 2, 0:16, width : width + LANES])
        tile = jnp.maximum(tile, lists[0, 3, 0:16, width : width + LANES]).astype(F32)
        flag_out[...] = jnp.where(iota(tile.shape, 1) == 2, tile, 0.0).astype(BF)
        me = y * BLOCKS + mine
        for i, o in enumerate(offsets):
            if i:
                copy = remote(flag_out, flag_in.at[me], flag_send.at[i], flag_recv.at[me], device_id=at(x, *plane(*o)))
                copy.start()
                flag_copies.append(copy)
        flag_in[me] = flag_out[...]

    scale = 1.0 / math.sqrt(tokens * 8)
    span = 512
    blocks = width // span
    out_copies = []

    def stream(i, slot):
        cols = pl.ds(pl.multiple_of(i * span, span), span)
        made = []
        for k in range(STEPS):
            there = pl.ds(pl.multiple_of((slot * STEPS + k) * span, span), span)
            made.append(
                pltpu.make_async_copy(
                    lists_hbm.at[:, k, :, :, cols], lists.at[:, :, :, there], out_sem.at[slot * STEPS + k]
                )
            )
        return made

    def gradients(first, last):
        def one(i, carry):
            slot = lax.rem(i, 2)
            cols = pl.ds(pl.multiple_of(i * span, span), span)

            @pl.when(i + 1 < blocks)
            def _():
                for copy in stream(i + 1, 1 - slot):
                    copy.start()

            for copy in stream(i, slot):
                copy.wait()
            total = jnp.zeros((2 * hid, span), F32)
            down = jnp.zeros((hid, span), F32)
            for k in range(STEPS):
                there = pl.ds(pl.multiple_of((slot * STEPS + k) * span, span), span)
                total = total + nn(turned[k, 0 : 2 * hid, 0:ROWS], lists[0, :, :, there].reshape(ROWS, span))
                down = down + nn(turned[k, 2 * hid : 3 * hid, 0:ROWS], lists[1, :, :, there].reshape(ROWS, span))
            total = total * scale
            w_gate[cols, :] = jnp.transpose(total[0:hid]).astype(BF)
            w_up[cols, :] = jnp.transpose(total[hid : 2 * hid]).astype(BF)
            w_down[:, cols] = (down * scale).astype(BF)
            return carry

        if first == 0:
            for copy in stream(0, 0):
                copy.start()
        lax.fori_loop(first, last, one, 0)
        rows = pl.ds(first * span, (last - first) * span)
        n = 8 + len(out_copies)
        made = [
            pltpu.make_async_copy(w_gate.at[rows], grad_gate_hbm.at[0, rows], out_sem.at[n]),
            pltpu.make_async_copy(w_up.at[rows], grad_up_hbm.at[0, rows], out_sem.at[n + 1]),
            pltpu.make_async_copy(w_down.at[:, rows], grad_down_hbm.at[0, :, rows], out_sem.at[n + 2]),
        ]
        for copy in made:
            copy.start()
        out_copies.extend(made)

    units_out(0)
    for copy in weights:
        copy.start()
    take_in(0)
    units_out(1)
    take_in(1)
    units_out(2)
    units_out(3)
    forward(0)
    take_in(2)
    share(0)
    forward(1)
    take_in(3)
    for copy in weights:
        copy.wait()
    compute(0)
    merge(0)
    share(1)
    forward(2)
    pass_on(0)
    send_back(0)
    compute(1)
    merge(1)
    share(2)
    forward(3)
    pass_on(1)
    send_back(1)
    compute(2)
    merge(2)
    share(3)
    pass_on(2)
    send_back(2)
    compute(3)
    tell()
    merge(3)
    gradients(0, 3)
    pass_on(3)
    gradients(3, 8)
    send_back(3)
    gradients(8, 14)

    for dy, dz, dc in offsets[1:]:
        ay, az, ac = plane(dy, dz, dc)
        j = ac * 16 + ay * 4 + az
        pltpu.make_async_copy(back.at[0, 0], returned_hbm.at[j], back_recv.at[j]).wait()
        j = ay * BLOCKS + az * 2 + ac
        pltpu.make_async_copy(flag_out, flag_in.at[j], flag_recv.at[j]).wait()
    pull = pltpu.make_async_copy(returned_hbm, arrived.at[:, :, pl.ds(0, full)], pull_sem.at[0])
    pull.start()
    seen = jnp.max(flag_in[...].astype(F32).reshape(32 * 16, LANES), axis=0, keepdims=True)
    overflow[...] = jnp.broadcast_to(jnp.max(seen, axis=1, keepdims=True), overflow.shape)
    pull.wait()
    for h in range(2):
        for first in range(0, half, 512):
            found = arrived[h * 16 : (h + 1) * 16, :, first : first + 512].reshape(2 * SLOTS, 512)
            moe_grad[:, h * half + first : h * half + first + 512] = nn(token_map, found).astype(BF)
    found = arrived[0:16, :, half:full].reshape(2 * SLOTS, LANES)
    gate_grad[...] = (nn(token_map, found) / gate).astype(BF)

    for copy in out_copies:
        copy.wait()
    for copy in unit_copies + flag_copies + [parts[STEPS - 1]]:
        copy.wait_send()
    for k in range(STEPS):
        for copy in own[k] + fwd[k] + twins[k]:
            copy.wait_send()
    for copy in far[STEPS - 1] + near[STEPS - 1] + backs[STEPS - 2] + backs[STEPS - 1]:
        copy.wait_send()


def fast(moe_input, out_grad, expert_ids, gate_values, w_gate, w_up, w_down):
    tokens, width = moe_input.shape
    hid = w_gate.shape[2]
    full = width // 2 + LANES
    vmem = pl.BlockSpec(memory_space=pltpu.VMEM)
    anywhere = pl.BlockSpec(memory_space=pl.ANY)
    dma = pltpu.SemaphoreType.DMA
    regular = pltpu.SemaphoreType.REGULAR
    return pl.pallas_call(
        kernel,
        out_shape=[
            jax.ShapeDtypeStruct((tokens, width), BF),
            jax.ShapeDtypeStruct((tokens, LANES), BF),
            jax.ShapeDtypeStruct((8, LANES), F32),
            jax.ShapeDtypeStruct(w_gate.shape, BF),
            jax.ShapeDtypeStruct(w_up.shape, BF),
            jax.ShapeDtypeStruct(w_down.shape, BF),
            jax.ShapeDtypeStruct((2, STEPS, 4, LIST, width + LANES), BF),
            jax.ShapeDtypeStruct((32, UNIT, full), BF),
        ],
        in_specs=[vmem] * 5 + [anywhere] * 3,
        out_specs=[vmem] * 3 + [anywhere] * 5,
        scratch_shapes=[
            pltpu.VMEM((width, hid), BF),
            pltpu.VMEM((width, hid), BF),
            pltpu.VMEM((hid, width), BF),
            pltpu.VMEM((2, 8, UNIT, width), BF),
            pltpu.VMEM((STEPS * BLOCKS, UNIT, width), BF),
            pltpu.VMEM((STEPS, LIST, width + LANES), BF),
            pltpu.VMEM((2, 4, LIST, width + LANES), BF),
            pltpu.VMEM((STEPS, LIST, SLOTS), BF),
            pltpu.VMEM((4, LIST, full), BF),
            pltpu.VMEM((4, LIST, full), BF),
            pltpu.VMEM((4, LIST, full), BF),
            pltpu.VMEM((2, LIST, full), BF),
            pltpu.VMEM((2, LIST, full), BF),
            pltpu.VMEM((2, BLOCKS, UNIT, full), BF),
            pltpu.VMEM((PADDED, 3 * hid), F32),
            pltpu.VMEM((ROWS, 2 * hid), BF),
            pltpu.VMEM((STEPS, 3 * hid, PADDED), BF),
            pltpu.VMEM((16, LANES), BF),
            pltpu.VMEM((32, 16, LANES), BF),
            dma((3,)),
            dma((32,)),
            dma((32,)),
            dma((STEPS, 3)),
            dma((STEPS, 2)),
            dma((STEPS, 2)),
            dma((STEPS, 2)),
            dma((STEPS, 4)),
            dma((STEPS, 4)),
            dma((STEPS,)),
            dma((STEPS,)),
            dma((STEPS, 2)),
            dma((STEPS, 2)),
            dma((STEPS, 2)),
            dma((STEPS, 2)),
            regular,
            regular,
            regular,
            dma((32,)),
            dma((32,)),
            dma((32,)),
            dma((32,)),
            dma((2,)),
            dma((17,)),
        ],
        compiler_params=pltpu.CompilerParams(
            collective_id=0, has_side_effects=True, vmem_limit_bytes=63 * 2**20
        ),
    )(moe_input, out_grad, expert_ids, expert_ids.reshape(1, tokens), gate_values, w_gate, w_up, w_down)


def silu_parts(value):
    sig = jax.nn.sigmoid(value)
    return (value * sig, sig * (1.0 + value * (1.0 - sig)))


def contract_rows(left, right):
    return lax.dot_general(
        left, right, (((0,), (0,)), ((), ())), preferred_element_type=jnp.float32
    )


def contract_cols(left, right):
    return lax.dot_general(
        left, right, (((1,), (1,)), ((), ())), preferred_element_type=jnp.float32
    )


def general(moe_input, out_grad, expert_ids, gate_values, w_gate, w_up, w_down):
    tok_rows = moe_input.shape[0]
    width = moe_input.shape[1]
    topw = expert_ids.shape[1]
    experts = lax.axis_size("ep")
    groups = lax.axis_size("fsdp")
    capacity = (3 * tok_rows * topw + experts - 1) // experts
    routes = tok_rows * topw
    flat_ids = expert_ids.reshape(routes)
    onehot = (flat_ids[:, None] == jnp.arange(experts, dtype=jnp.int32)[None, :]).astype(jnp.int32)
    earlier = jnp.cumsum(onehot, axis=0) - onehot
    slot_index = jnp.sum(earlier * onehot, axis=1)
    target = flat_ids * capacity + slot_index
    placing = (jnp.arange(experts * capacity, dtype=jnp.int32)[:, None] == target[None, :]).astype(
        jnp.bfloat16
    )
    route_input = jnp.repeat(moe_input, topw, axis=0)
    route_grad = jnp.repeat(out_grad, topw, axis=0)
    send_input = (
        jnp.dot(placing, route_input, preferred_element_type=jnp.float32)
        .astype(jnp.bfloat16)
        .reshape(experts, capacity, width)
    )
    send_grad = (
        jnp.dot(placing, route_grad, preferred_element_type=jnp.float32)
        .astype(jnp.bfloat16)
        .reshape(experts, capacity, width)
    )
    send_gate = jnp.sum(
        placing.astype(jnp.float32) * gate_values.reshape(1, routes).astype(jnp.float32), axis=1
    )
    send_gate = send_gate.astype(jnp.bfloat16).reshape(experts, capacity)
    recv_input, recv_grad, recv_gate = (
        lax.all_to_all(send_input, "ep", split_axis=0, concat_axis=0, tiled=True),
        lax.all_to_all(send_grad, "ep", split_axis=0, concat_axis=0, tiled=True),
        lax.all_to_all(send_gate, "ep", split_axis=0, concat_axis=0, tiled=True),
    )
    weight_gate = w_gate[0]
    weight_up = w_up[0]
    weight_down = w_down[0]
    expert_scale = 1.0 / math.sqrt(tok_rows * groups)
    gate_scale = 1.0 / math.sqrt(width)
    piece_input = lax.all_gather(recv_input, "fsdp", axis=0, tiled=True)
    piece_grad = lax.all_gather(recv_grad, "fsdp", axis=0, tiled=True)
    piece_gate = lax.all_gather(recv_gate, "fsdp", axis=0, tiled=True)
    count = piece_input.shape[0] * piece_input.shape[1]
    rows_in = piece_input.reshape(count, width)
    rows_grad = piece_grad.reshape(count, width)
    gates = piece_gate.reshape(count, 1).astype(jnp.float32)
    pre_gate = jnp.dot(rows_in, weight_gate, preferred_element_type=jnp.float32)
    pre_up = jnp.dot(rows_in, weight_up, preferred_element_type=jnp.float32)
    act, slope = silu_parts(pre_gate)
    hidden = (act * pre_up).astype(jnp.bfloat16)
    raw = contract_cols(rows_grad, weight_down)
    scaled = gates * raw
    grad_pre_gate = (scaled * pre_up * slope).astype(jnp.bfloat16)
    grad_pre_up = (scaled * act).astype(jnp.bfloat16)
    gated_grad = (gates * rows_grad.astype(jnp.float32)).astype(jnp.bfloat16)
    acc_gate = contract_rows(rows_in, grad_pre_gate)
    acc_up = contract_rows(rows_in, grad_pre_up)
    acc_down = contract_rows(hidden, gated_grad)
    rows_back = contract_cols(grad_pre_gate, weight_gate) + contract_cols(grad_pre_up, weight_up)
    gate_back = jnp.sum(hidden.astype(jnp.float32) * raw, axis=1) * gate_scale
    part_rows = rows_back
    part_gate = gate_back
    acc_gate, acc_up, acc_down, part_rows, part_gate = (
        acc_gate,
        acc_up,
        acc_down,
        part_rows,
        part_gate,
    )
    grad_w_gate = (acc_gate * expert_scale).astype(jnp.bfloat16)[None]
    grad_w_up = (acc_up * expert_scale).astype(jnp.bfloat16)[None]
    grad_w_down = (acc_down * expert_scale).astype(jnp.bfloat16)[None]
    summed_rows, summed_gate = (
        lax.psum_scatter(
            part_rows.astype(jnp.bfloat16), "fsdp", scatter_dimension=0, tiled=True
        ).astype(jnp.float32),
        lax.psum_scatter(
            part_gate.astype(jnp.bfloat16), "fsdp", scatter_dimension=0, tiled=True
        ).astype(jnp.float32),
    )
    back_rows = summed_rows.astype(jnp.bfloat16).reshape(experts, capacity, width)
    back_gate = summed_gate.astype(jnp.bfloat16).reshape(experts, capacity)
    ret_rows, ret_gate = (
        lax.all_to_all(back_rows, "ep", split_axis=0, concat_axis=0, tiled=True),
        lax.all_to_all(back_gate, "ep", split_axis=0, concat_axis=0, tiled=True),
    )
    flat_rows = ret_rows.reshape(experts * capacity, width)
    route_back = contract_rows(placing, flat_rows)
    moe_grad = jnp.sum(route_back.reshape(tok_rows, topw, width), axis=1).astype(jnp.bfloat16)
    gate_back = jnp.sum(
        placing.astype(jnp.float32) * ret_gate.reshape(experts * capacity, 1).astype(jnp.float32),
        axis=0,
    )
    gate_grad = gate_back.reshape(tok_rows, topw).astype(jnp.bfloat16)
    return (moe_grad, gate_grad, grad_w_gate, grad_w_up, grad_w_down)


def body(*args):
    moe_grad, gate_wide, overflow, grad_gate, grad_up, grad_down, _, _ = fast(*args)
    made = (moe_grad, gate_wide[:, 0:1], grad_gate, grad_up, grad_down)
    return lax.cond(overflow[0, 0] > 0.0, lambda: general(*args), lambda: made)


def solution(mesh):
    rows = P(("ep", "fsdp"), None)
    columns = P("ep", None, "fsdp")
    return jax.shard_map(
        body,
        mesh=mesh,
        in_specs=(rows, rows, rows, rows, columns, columns, P("ep", "fsdp", None)),
        out_specs=(rows, rows, columns, columns, P("ep", "fsdp", None)),
        check_vma=False,
    )
```

```python
import functools
import math

import jax
import jax.numpy as jnp
from jax import lax
from jax.experimental import pallas as pl
from jax.experimental.pallas import tpu as pltpu
from jax.sharding import PartitionSpec as P

BF = jnp.bfloat16
F32 = jnp.float32
CAP = 7
UNIT = 16
FLAG_ROW = 2 * CAP
STEPS = 4
BLOCKS = 8
SLOTS = BLOCKS * UNIT
LIST = 80
ROWS = 4 * LIST
PADDED = 384
LANES = 128
MESH = pl.DeviceIdType.MESH


def nn(left, right):
    return jnp.dot(left, right, preferred_element_type=F32)


def nt(left, right):
    return lax.dot_general(left, right, (((1,), (1,)), ((), ())), preferred_element_type=F32)


def tn(left, right):
    return lax.dot_general(left, right, (((0,), (0,)), ((), ())), preferred_element_type=F32)


def iota(shape, dim):
    return lax.broadcasted_iota(jnp.int32, shape, dim)


def ones(where):
    return where.astype(F32).astype(BF)


def kernel(
    moe_input, out_grad, ids, gates, w_gate_hbm, w_up_hbm, w_down_hbm,
    moe_grad, gate_grad, overflow, grad_gate_hbm, grad_up_hbm, grad_down_hbm, lists_hbm, returned_hbm,
    w_gate, w_up, w_down, units, relay, arrived, dense, lists, picks, all_part, twin_out, twin_in, far_in, near_in, back,
    acc, packed, turned, flag_out, flag_in,
    w_sem, y_send, y_recv, unit_send, unit_recv, own_send, own_recv, fwd_send, fwd_recv, twin_send, twin_recv,
    part_send, part_recv, far_send, far_recv, near_send, near_recv, part_free, far_free, near_free,
    back_send, back_recv, flag_send, flag_recv, pull_sem, out_sem,
):
    tokens, width = moe_input.shape
    hid = w_gate.shape[1]
    half = width // 2
    full = half + LANES
    ep = lax.axis_index("ep")
    fs = lax.axis_index("fsdp")
    z = lax.rem(fs, 2) * 2 + ep // 8
    y = lax.rem(ep // 2, 4)
    core = lax.rem(ep, 2)
    x = fs // 2
    mine = z * 2 + core
    other = 1 - core

    def at(ax, ay, az, ac):
        return (lax.rem(az, 2) * 8 + ay * 2 + ac, ax * 2 + az // 2)

    def shift(v, n):
        return lax.rem(v + n, 4)

    plus = at(shift(x, 1), y, z, core)
    minus = at(shift(x, 3), y, z, core)
    twin = at(x, y, z, other)
    remote = functools.partial(pltpu.make_async_remote_copy, device_id_type=MESH)
    offsets = [(dy, dz, dc) for dy in range(4) for dz in range(4) for dc in range(2)]

    def plane(dy, dz, dc):
        return shift(y, dy), shift(z, dz), lax.rem(core + dc, 2)

    weights = [
        pltpu.make_async_copy(w_gate_hbm.at[0], w_gate, w_sem.at[0]),
        pltpu.make_async_copy(w_up_hbm.at[0], w_up, w_sem.at[1]),
        pltpu.make_async_copy(w_down_hbm.at[0], w_down, w_sem.at[2]),
    ]
    for copy in weights:
        copy.start()
    barrier = pltpu.get_barrier_semaphore()
    partners = [plus, minus] + [at(x, *plane(*o)) for o in offsets[1:]]
    for partner in partners:
        pl.semaphore_signal(barrier, 1, device_id=partner, device_id_type=MESH)

    token_square = (tokens, tokens)
    diagonal = iota(token_square, 0) == iota(token_square, 1)

    def upright(row):
        return jnp.sum(jnp.where(diagonal, row, 0.0), axis=1, keepdims=True)

    row_id = ids[...]
    col_id = upright(row_id.astype(F32)).astype(jnp.int32)
    same = col_id == row_id
    above = iota((tokens, tokens), 0) < iota((tokens, tokens), 1)
    below = iota((tokens, tokens), 0) > iota((tokens, tokens), 1)
    slot_row = jnp.sum((same & above).astype(F32), axis=0, keepdims=True).astype(jnp.int32)
    slot_col = jnp.sum((same & below).astype(F32), axis=1, keepdims=True).astype(jnp.int32)
    target = ((row_id // 2) % 4 * 2 + row_id // 8) * UNIT + (row_id % 2) * CAP + slot_row
    place = (iota((SLOTS, tokens), 0) == target).astype(F32)
    taken = jnp.sum(place, axis=1, keepdims=True)
    place = place.astype(BF)
    square = (SLOTS, SLOTS)
    spread = ones(iota(square, 1) == mine * UNIT + iota(square, 0) % UNIT)
    to_flag = ones(
        (iota(square, 0) % UNIT == FLAG_ROW) & (iota(square, 0) // UNIT == iota(square, 1) // UNIT)
    )
    flags = nn(to_flag, (taken * spread.astype(F32)).astype(BF))
    gate = upright(gates[...].astype(F32))
    step = 1024

    def pack(i, carry):
        cols = pl.ds(pl.multiple_of(i * step, step), step)
        gated = (gate * out_grad[:, cols].astype(F32)).astype(BF)
        units[:, 0, :, :, cols] = nn(place, moe_input[:, cols]).astype(BF).reshape(4, 2, UNIT, step)
        units[:, 1, :, :, cols] = nn(place, gated).astype(BF).reshape(4, 2, UNIT, step)
        return carry

    lax.fori_loop(0, width // step, pack, 0)
    for a in range(2):
        head = units[:, a, :, :, 0:LANES].reshape(SLOTS, LANES).astype(F32)
        units[:, a, :, :, 0:LANES] = (head + flags).astype(BF).reshape(4, 2, UNIT, LANES)
    from_pair = iota((tokens, 2 * SLOTS), 1)
    token_map = ones(
        (from_pair // 64 == (col_id // 2) % 4)
        & ((from_pair // UNIT) % 2 == col_id // 8)
        & (from_pair % UNIT == (col_id % 2) * CAP + slot_col)
    )
    pl.semaphore_wait(barrier, len(partners))

    unit_copies = []

    over_y = {}

    def units_over(k):
        ay = shift(y, 4 - k)
        over_y[k] = remote(units.at[ay], relay.at[k - 1], y_send.at[k], y_recv.at[k], device_id=at(x, ay, z, core))
        over_y[k].start()
        unit_copies.append(over_y[k])

    def units_out(k):
        if k:
            over_y[k].wait_recv()
        for dz in range(4):
            for dc in range(2):
                _, az, ac = plane(0, dz, dc)
                low = lax.rem(az, 2)
                src = relay.at[k - 1, ac, low] if k else units.at[y, ac, low]
                dst = arrived.at[k * BLOCKS + mine]
                index = (k * 4 + dz) * 2 + dc
                sem = unit_recv.at[k * BLOCKS + mine]
                if dz or dc:
                    copy = remote(src, dst, unit_send.at[index], sem, device_id=at(x, y, az, ac))
                    copy.start()
                    unit_copies.append(copy)
                else:
                    pltpu.make_async_copy(src, dst, sem).start()

    earlier = ones(iota(square, 0) < iota(square, 1))
    owner = iota(square, 0) % UNIT
    lane = iota(square, 1)
    whose = ones(((lane == 0) & (owner < CAP)) | ((lane == 1) & (owner >= CAP) & (owner < 2 * CAP)))
    own, kept, fwd, twins, parts, far, near, backs = ({} for _ in range(8))
    over = [jnp.zeros((1, 1), F32)]

    def take_in(k):
        for b in range(BLOCKS):
            j = k * BLOCKS + b
            pltpu.make_async_copy(arrived.at[j], arrived.at[j], unit_recv.at[j]).wait()
        tiles = arrived[k * BLOCKS : (k + 1) * BLOCKS, :, 0:LANES].astype(F32)
        flag = jnp.where(iota(tiles.shape, 1) == FLAG_ROW, tiles, 0.0)
        flag = jnp.sum(flag.reshape(SLOTS, LANES), axis=0, keepdims=True)
        rank = nn(flag.astype(BF), earlier)
        count = jnp.sum(flag, axis=1, keepdims=True)
        over[0] = jnp.maximum(over[0], (count > LIST).astype(F32))
        pick = ones((iota((LIST, SLOTS), 0).astype(F32) == rank) & (flag > 0.5))
        picks[k] = pick
        masks = nn(pick, whose) + jnp.where(iota((LIST, LANES), 1) == 2, over[0], 0.0)
        dense[k, :, width : width + LANES] = masks.astype(BF)

        def move(i, carry):
            cols = pl.ds(pl.multiple_of(i * step, step), step)
            found = arrived[k * BLOCKS : (k + 1) * BLOCKS, :, cols].reshape(SLOTS, step)
            dense[k, :, cols] = nn(pick, found).astype(BF)
            return carry

        lax.fori_loop(0, width // step, move, 0)
        to = lists_hbm.at[core, k]
        own[k] = [
            remote(dense.at[k], to.at[1], own_send.at[k, 0], own_recv.at[k, 0], device_id=plus),
            remote(dense.at[k], to.at[2], own_send.at[k, 1], own_recv.at[k, 1], device_id=minus),
        ]
        twins[k] = [remote(dense.at[k], to.at[0], twin_send.at[k, 0], twin_recv.at[k, 0], device_id=twin)]
        kept[k] = pltpu.make_async_copy(dense.at[k], to.at[0], own_send.at[k, 2])
        for copy in own[k] + twins[k] + [kept[k]]:
            copy.start()

    def forward(k):
        to = lists_hbm.at[core, k]
        cut = 48 if k % 2 == 0 else 32
        low, high = pl.ds(0, cut), pl.ds(cut, LIST - cut)
        fwd[k] = [
            remote(to.at[1, low], to.at[3, low], fwd_send.at[k, 0], fwd_recv.at[k, 0], device_id=plus),
            remote(to.at[2, high], to.at[3, high], fwd_send.at[k, 1], fwd_recv.at[k, 1], device_id=minus),
        ]
        for i in range(2):
            own[k][i].wait_recv()
            fwd[k][i].start()
            copy = remote(to.at[i + 1], to.at[i + 1], twin_send.at[k, i + 1], twin_recv.at[k, i + 1], device_id=twin)
            copy.start()
            twins[k].append(copy)

    def share(k):
        to = lists_hbm.at[core, k]
        for copy in fwd[k]:
            copy.wait_recv()
        copy = remote(to.at[3], to.at[3], twin_send.at[k, 3], twin_recv.at[k, 3], device_id=twin)
        copy.start()
        twins[k].append(copy)

    def compute(k):
        kept[k].wait()
        for copy in twins[k]:
            copy.wait_recv()
        pull = pltpu.make_async_copy(lists_hbm.at[:, k], lists, pull_sem.at[0])
        pull.start()
        acc[...] = jnp.zeros_like(acc)
        pull.wait()

        def gather(i, carry):
            cols = pl.ds(pl.multiple_of(i * step, step), step)
            left = lists[0, :, :, cols].reshape(ROWS, step)
            acc[0:ROWS, 0:hid] += nn(left, w_gate[cols, :])
            acc[0:ROWS, hid : 2 * hid] += nn(left, w_up[cols, :])
            acc[0:ROWS, 2 * hid : 3 * hid] += nt(lists[1, :, :, cols].reshape(ROWS, step), w_down[:, cols])
            return carry

        lax.fori_loop(0, width // step, gather, 0)
        part = all_part.at[k % 3]
        if k:
            parts[k - 1].wait_send()
        if k >= 3:
            for copy in far[k - 3] + near[k - 3]:
                copy.wait_send()
        for r in range(4):
            rows = slice(r * LIST, (r + 1) * LIST)
            tile = lists[0, r, :, width : width + LANES].astype(F32)
            mask = jnp.sum(jnp.where(iota(tile.shape, 1) == core, tile, 0.0), axis=1, keepdims=True)
            pre_gate = acc[rows, 0:hid]
            pre_up = acc[rows, hid : 2 * hid]
            scaled = acc[rows, 2 * hid : 3 * hid] * mask
            sig = jax.nn.sigmoid(pre_gate)
            act = pre_gate * sig
            slope = sig * (1.0 + pre_gate * (1.0 - sig))
            hidden = (act * pre_up).astype(BF).astype(F32) * mask
            piece = jnp.sum(hidden * scaled, axis=1, keepdims=True) * (1.0 / math.sqrt(width))
            acc[rows, 0:hid] = scaled * pre_up * slope
            acc[rows, hid : 2 * hid] = scaled * act
            acc[rows, 2 * hid : 3 * hid] = hidden
            wide = jnp.broadcast_to(piece, (LIST, LANES)).astype(BF)
            part[r, :, half:full] = wide
            twin_out[r, :, half:full] = wide
        turned[k] = jnp.transpose(acc[...]).astype(BF)
        packed[...] = acc[0:ROWS, 0 : 2 * hid].astype(BF)
        span = 512

        def rows_back(into, first):
            def one(i, carry):
                cols = pl.ds(pl.multiple_of(i * span, span), span)
                here = pl.ds(pl.multiple_of(first + i * span, span), span)
                total = nt(packed[:, 0:hid], w_gate[here, :]) + nt(packed[:, hid : 2 * hid], w_up[here, :])
                into[:, :, cols] = total.astype(BF).reshape(4, LIST, span)
                return carry

            lax.fori_loop(0, half // span, one, 0)

        rows_back(twin_out, other * half)
        if k:
            pl.semaphore_wait(part_free, 1)
        parts[k] = remote(twin_out, twin_in, part_send.at[k], part_recv.at[k], device_id=twin)
        parts[k].start()
        rows_back(part, core * half)

    def merge(k):
        part = all_part.at[k % 3]
        parts[k].wait_recv()

        def add(r, carry):
            part[r] = (part[r].astype(F32) + twin_in[r].astype(F32)).astype(BF)
            return carry

        cut = 48 if k % 2 == 0 else 32
        low, high = pl.ds(0, cut), pl.ds(cut, LIST - cut)
        part[3] = (part[3].astype(F32) + twin_in[3].astype(F32)).astype(BF)
        if k:
            pl.semaphore_wait(far_free, 2)
        far[k] = [
            remote(part.at[3, low], far_in.at[0, low], far_send.at[k, 0], far_recv.at[k, 0], device_id=plus),
            remote(part.at[3, high], far_in.at[1, high], far_send.at[k, 1], far_recv.at[k, 1], device_id=minus),
        ]
        for copy in far[k]:
            copy.start()
        lax.fori_loop(0, 3, add, 0)
        if k < STEPS - 1:
            pl.semaphore_signal(part_free, 1, device_id=twin, device_id_type=MESH)

    def pass_on(k):
        part = all_part.at[k % 3]
        if k:
            pl.semaphore_wait(near_free, 2)
        near[k] = [
            remote(part.at[2], near_in.at[0], near_send.at[k, 0], near_recv.at[k, 0], device_id=plus),
            remote(part.at[1], near_in.at[1], near_send.at[k, 1], near_recv.at[k, 1], device_id=minus),
        ]
        cut = 48 if k % 2 == 0 else 32
        for i, rel, rows, giver in ((0, 2, slice(0, cut), minus), (1, 1, slice(cut, LIST), plus)):
            far[k][i].wait_recv()
            part[rel, rows] = (part[rel, rows].astype(F32) + far_in[i, rows].astype(F32)).astype(BF)
            if k < STEPS - 1:
                pl.semaphore_signal(far_free, 1, device_id=giver, device_id_type=MESH)
            near[k][i].start()

    def send_back(k):
        part = all_part.at[k % 3]
        for copy in near[k]:
            copy.wait_recv()
        slot = k % 2
        if k >= 2:
            for copy in backs[k - 2]:
                copy.wait_send()
        for first in range(0, full, 1024):
            cols = slice(first, min(first + 1024, full))
            total = tn(picks[k], part[0, :, cols]) + tn(picks[k], near_in[0, :, cols])
            total = total + tn(picks[k], near_in[1, :, cols])
            back[slot, :, :, cols] = total.astype(BF).reshape(BLOCKS, UNIT, cols.stop - cols.start)
        if k < STEPS - 1:
            for giver in (minus, plus):
                pl.semaphore_signal(near_free, 1, device_id=giver, device_id_type=MESH)
        me = core * 16 + y * 4 + z
        backs[k] = []
        for dz in range(4):
            for dc in range(2):
                ay, az, ac = plane(k, dz, dc)
                src = back.at[slot, az * 2 + ac]
                index = (k * 4 + dz) * 2 + dc
                if k or dz or dc:
                    copy = remote(src, returned_hbm.at[me], back_send.at[index], back_recv.at[me], device_id=at(x, ay, az, ac))
                    copy.start()
                    backs[k].append(copy)
                else:
                    stay = pltpu.make_async_copy(src, returned_hbm.at[me], pull_sem.at[1])
                    stay.start()
                    stay.wait()

    flag_copies = []

    def tell():
        tile = jnp.maximum(lists[0, 0, 0:16, width : width + LANES], lists[0, 1, 0:16, width : width + LANES])
        tile = jnp.maximum(tile, lists[0, 2, 0:16, width : width + LANES])
        tile = jnp.maximum(tile, lists[0, 3, 0:16, width : width + LANES]).astype(F32)
        flag_out[...] = jnp.where(iota(tile.shape, 1) == 2, tile, 0.0).astype(BF)
        me = y * BLOCKS + mine
        for i, o in enumerate(offsets):
            if i:
                copy = remote(flag_out, flag_in.at[me], flag_send.at[i], flag_recv.at[me], device_id=at(x, *plane(*o)))
                copy.start()
                flag_copies.append(copy)
        flag_in[me] = flag_out[...]

    scale = 1.0 / math.sqrt(tokens * 8)
    span = 512
    blocks = width // span
    out_copies = []

    def stream(i, slot):
        cols = pl.ds(pl.multiple_of(i * span, span), span)
        made = []
        for k in range(STEPS):
            there = pl.ds(pl.multiple_of((slot * STEPS + k) * span, span), span)
            made.append(
                pltpu.make_async_copy(
                    lists_hbm.at[:, k, :, :, cols], lists.at[:, :, :, there], out_sem.at[slot * STEPS + k]
                )
            )
        return made

    def gradients(first, last):
        def one(i, carry):
            slot = lax.rem(i, 2)
            cols = pl.ds(pl.multiple_of(i * span, span), span)

            @pl.when(i + 1 < blocks)
            def _():
                for copy in stream(i + 1, 1 - slot):
                    copy.start()

            for copy in stream(i, slot):
                copy.wait()
            total = jnp.zeros((2 * hid, span), F32)
            down = jnp.zeros((hid, span), F32)
            for k in range(STEPS):
                there = pl.ds(pl.multiple_of((slot * STEPS + k) * span, span), span)
                total = total + nn(turned[k, 0 : 2 * hid, 0:ROWS], lists[0, :, :, there].reshape(ROWS, span))
                down = down + nn(turned[k, 2 * hid : 3 * hid, 0:ROWS], lists[1, :, :, there].reshape(ROWS, span))
            total = total * scale
            w_gate[cols, :] = jnp.transpose(total[0:hid]).astype(BF)
            w_up[cols, :] = jnp.transpose(total[hid : 2 * hid]).astype(BF)
            w_down[:, cols] = (down * scale).astype(BF)
            return carry

        if first == 0:
            for copy in stream(0, 0):
                copy.start()
        lax.fori_loop(first, last, one, 0)
        rows = pl.ds(first * span, (last - first) * span)
        n = 8 + len(out_copies)
        made = [
            pltpu.make_async_copy(w_gate.at[rows], grad_gate_hbm.at[0, rows], out_sem.at[n]),
            pltpu.make_async_copy(w_up.at[rows], grad_up_hbm.at[0, rows], out_sem.at[n + 1]),
            pltpu.make_async_copy(w_down.at[:, rows], grad_down_hbm.at[0, :, rows], out_sem.at[n + 2]),
        ]
        for copy in made:
            copy.start()
        out_copies.extend(made)

    units_out(0)
    for k in range(1, STEPS):
        units_over(k)
    take_in(0)
    units_out(1)
    take_in(1)
    units_out(2)
    forward(0)
    take_in(2)
    units_out(3)
    forward(1)
    share(0)
    take_in(3)
    for copy in weights:
        copy.wait()
    compute(0)
    merge(0)
    share(1)
    forward(2)
    compute(1)
    pass_on(0)
    merge(1)
    share(2)
    forward(3)
    compute(2)
    send_back(0)
    pass_on(1)
    merge(2)
    share(3)
    compute(3)
    tell()
    send_back(1)
    pass_on(2)
    merge(3)
    gradients(0, 3)
    send_back(2)
    pass_on(3)
    gradients(3, 8)
    send_back(3)
    gradients(8, 14)

    for dy, dz, dc in offsets[1:]:
        ay, az, ac = plane(dy, dz, dc)
        j = ac * 16 + ay * 4 + az
        pltpu.make_async_copy(back.at[0, 0], returned_hbm.at[j], back_recv.at[j]).wait()
        j = ay * BLOCKS + az * 2 + ac
        pltpu.make_async_copy(flag_out, flag_in.at[j], flag_recv.at[j]).wait()
    pull = pltpu.make_async_copy(returned_hbm, arrived.at[:, :, pl.ds(0, full)], pull_sem.at[0])
    pull.start()
    seen = jnp.max(flag_in[...].astype(F32).reshape(32 * 16, LANES), axis=0, keepdims=True)
    overflow[...] = jnp.broadcast_to(jnp.max(seen, axis=1, keepdims=True), overflow.shape)
    pull.wait()
    for h in range(2):
        for first in range(0, half, 512):
            found = arrived[h * 16 : (h + 1) * 16, :, first : first + 512].reshape(2 * SLOTS, 512)
            moe_grad[:, h * half + first : h * half + first + 512] = nn(token_map, found).astype(BF)
    found = arrived[0:16, :, half:full].reshape(2 * SLOTS, LANES)
    sums = nn(token_map, found)[:, 0:1] / gate
    gate_grad[...] = jnp.sum(jnp.where(diagonal, sums, 0.0), axis=0, keepdims=True).astype(BF)

    for copy in out_copies:
        copy.wait()
    for copy in unit_copies + flag_copies + [parts[STEPS - 1]]:
        copy.wait_send()
    for k in range(STEPS):
        for copy in own[k] + fwd[k] + twins[k]:
            copy.wait_send()
    for k in range(STEPS - 3, STEPS):
        for copy in far[k] + near[k]:
            copy.wait_send()
    for copy in backs[STEPS - 2] + backs[STEPS - 1]:
        copy.wait_send()


def fast(moe_input, out_grad, expert_ids, gate_values, w_gate, w_up, w_down):
    tokens, width = moe_input.shape
    hid = w_gate.shape[2]
    full = width // 2 + LANES
    vmem = pl.BlockSpec(memory_space=pltpu.VMEM)
    anywhere = pl.BlockSpec(memory_space=pl.ANY)
    dma = pltpu.SemaphoreType.DMA
    regular = pltpu.SemaphoreType.REGULAR
    return pl.pallas_call(
        kernel,
        out_shape=[
            jax.ShapeDtypeStruct((tokens, width), BF),
            jax.ShapeDtypeStruct((1, tokens), BF),
            jax.ShapeDtypeStruct((8, LANES), F32),
            jax.ShapeDtypeStruct(w_gate.shape, BF),
            jax.ShapeDtypeStruct(w_up.shape, BF),
            jax.ShapeDtypeStruct(w_down.shape, BF),
            jax.ShapeDtypeStruct((2, STEPS, 4, LIST, width + LANES), BF),
            jax.ShapeDtypeStruct((32, UNIT, full), BF),
        ],
        in_specs=[vmem] * 4 + [anywhere] * 3,
        out_specs=[vmem] * 3 + [anywhere] * 5,
        scratch_shapes=[
            pltpu.VMEM((width, hid), BF),
            pltpu.VMEM((width, hid), BF),
            pltpu.VMEM((hid, width), BF),
            pltpu.VMEM((4, 2, 2, UNIT, width), BF),
            pltpu.VMEM((STEPS - 1, 2, 2, UNIT, width), BF),
            pltpu.VMEM((STEPS * BLOCKS, UNIT, width), BF),
            pltpu.VMEM((STEPS, LIST, width + LANES), BF),
            pltpu.VMEM((2, 4, LIST, width + LANES), BF),
            pltpu.VMEM((STEPS, LIST, SLOTS), BF),
            pltpu.VMEM((3, 4, LIST, full), BF),
            pltpu.VMEM((4, LIST, full), BF),
            pltpu.VMEM((4, LIST, full), BF),
            pltpu.VMEM((2, LIST, full), BF),
            pltpu.VMEM((2, LIST, full), BF),
            pltpu.VMEM((2, BLOCKS, UNIT, full), BF),
            pltpu.VMEM((PADDED, 3 * hid), F32),
            pltpu.VMEM((ROWS, 2 * hid), BF),
            pltpu.VMEM((STEPS, 3 * hid, PADDED), BF),
            pltpu.VMEM((16, LANES), BF),
            pltpu.VMEM((32, 16, LANES), BF),
            dma((3,)),
            dma((STEPS,)),
            dma((STEPS,)),
            dma((32,)),
            dma((32,)),
            dma((STEPS, 3)),
            dma((STEPS, 2)),
            dma((STEPS, 2)),
            dma((STEPS, 2)),
            dma((STEPS, 4)),
            dma((STEPS, 4)),
            dma((STEPS,)),
            dma((STEPS,)),
            dma((STEPS, 2)),
            dma((STEPS, 2)),
            dma((STEPS, 2)),
            dma((STEPS, 2)),
            regular,
            regular,
            regular,
            dma((32,)),
            dma((32,)),
            dma((32,)),
            dma((32,)),
            dma((2,)),
            dma((17,)),
        ],
        compiler_params=pltpu.CompilerParams(
            collective_id=0, has_side_effects=True, vmem_limit_bytes=63 * 2**20
        ),
    )(moe_input, out_grad, expert_ids.reshape(1, tokens), gate_values.reshape(1, tokens), w_gate, w_up, w_down)


def silu_parts(value):
    sig = jax.nn.sigmoid(value)
    return (value * sig, sig * (1.0 + value * (1.0 - sig)))


def contract_rows(left, right):
    return lax.dot_general(
        left, right, (((0,), (0,)), ((), ())), preferred_element_type=jnp.float32
    )


def contract_cols(left, right):
    return lax.dot_general(
        left, right, (((1,), (1,)), ((), ())), preferred_element_type=jnp.float32
    )


def general(moe_input, out_grad, expert_ids, gate_values, w_gate, w_up, w_down):
    tok_rows = moe_input.shape[0]
    width = moe_input.shape[1]
    topw = expert_ids.shape[1]
    experts = lax.axis_size("ep")
    groups = lax.axis_size("fsdp")
    capacity = (3 * tok_rows * topw + experts - 1) // experts
    routes = tok_rows * topw
    flat_ids = expert_ids.reshape(routes)
    onehot = (flat_ids[:, None] == jnp.arange(experts, dtype=jnp.int32)[None, :]).astype(jnp.int32)
    earlier = jnp.cumsum(onehot, axis=0) - onehot
    slot_index = jnp.sum(earlier * onehot, axis=1)
    target = flat_ids * capacity + slot_index
    placing = (jnp.arange(experts * capacity, dtype=jnp.int32)[:, None] == target[None, :]).astype(
        jnp.bfloat16
    )
    route_input = jnp.repeat(moe_input, topw, axis=0)
    route_grad = jnp.repeat(out_grad, topw, axis=0)
    send_input = (
        jnp.dot(placing, route_input, preferred_element_type=jnp.float32)
        .astype(jnp.bfloat16)
        .reshape(experts, capacity, width)
    )
    send_grad = (
        jnp.dot(placing, route_grad, preferred_element_type=jnp.float32)
        .astype(jnp.bfloat16)
        .reshape(experts, capacity, width)
    )
    send_gate = jnp.sum(
        placing.astype(jnp.float32) * gate_values.reshape(1, routes).astype(jnp.float32), axis=1
    )
    send_gate = send_gate.astype(jnp.bfloat16).reshape(experts, capacity)
    recv_input, recv_grad, recv_gate = (
        lax.all_to_all(send_input, "ep", split_axis=0, concat_axis=0, tiled=True),
        lax.all_to_all(send_grad, "ep", split_axis=0, concat_axis=0, tiled=True),
        lax.all_to_all(send_gate, "ep", split_axis=0, concat_axis=0, tiled=True),
    )
    weight_gate = w_gate[0]
    weight_up = w_up[0]
    weight_down = w_down[0]
    expert_scale = 1.0 / math.sqrt(tok_rows * groups)
    gate_scale = 1.0 / math.sqrt(width)

    def gathered(own):
        copies = jnp.broadcast_to(own[None], (groups,) + own.shape)
        copies = lax.all_to_all(copies, "fsdp", split_axis=0, concat_axis=0, tiled=True)
        return copies.reshape((groups * own.shape[0],) + own.shape[1:])

    def summed(pieces):
        spread = lax.all_to_all(pieces, "fsdp", split_axis=0, concat_axis=0, tiled=True)
        spread = spread.reshape((groups, pieces.shape[0] // groups) + pieces.shape[1:])
        return jnp.sum(spread.astype(jnp.float32), axis=0)

    piece_input = gathered(recv_input)
    piece_grad = gathered(recv_grad)
    piece_gate = gathered(recv_gate)
    count = piece_input.shape[0] * piece_input.shape[1]
    rows_in = piece_input.reshape(count, width)
    rows_grad = piece_grad.reshape(count, width)
    gates = piece_gate.reshape(count, 1).astype(jnp.float32)
    pre_gate = jnp.dot(rows_in, weight_gate, preferred_element_type=jnp.float32)
    pre_up = jnp.dot(rows_in, weight_up, preferred_element_type=jnp.float32)
    act, slope = silu_parts(pre_gate)
    hidden = (act * pre_up).astype(jnp.bfloat16)
    raw = contract_cols(rows_grad, weight_down)
    scaled = gates * raw
    grad_pre_gate = (scaled * pre_up * slope).astype(jnp.bfloat16)
    grad_pre_up = (scaled * act).astype(jnp.bfloat16)
    gated_grad = (gates * rows_grad.astype(jnp.float32)).astype(jnp.bfloat16)
    acc_gate = contract_rows(rows_in, grad_pre_gate)
    acc_up = contract_rows(rows_in, grad_pre_up)
    acc_down = contract_rows(hidden, gated_grad)
    rows_back = contract_cols(grad_pre_gate, weight_gate) + contract_cols(grad_pre_up, weight_up)
    gate_back = jnp.sum(hidden.astype(jnp.float32) * raw, axis=1) * gate_scale
    part_rows = rows_back
    part_gate = gate_back
    acc_gate, acc_up, acc_down, part_rows, part_gate = (
        acc_gate,
        acc_up,
        acc_down,
        part_rows,
        part_gate,
    )
    grad_w_gate = (acc_gate * expert_scale).astype(jnp.bfloat16)[None]
    grad_w_up = (acc_up * expert_scale).astype(jnp.bfloat16)[None]
    grad_w_down = (acc_down * expert_scale).astype(jnp.bfloat16)[None]
    summed_rows = summed(part_rows.astype(jnp.bfloat16))
    summed_gate = summed(part_gate.astype(jnp.bfloat16))
    back_rows = summed_rows.astype(jnp.bfloat16).reshape(experts, capacity, width)
    back_gate = summed_gate.astype(jnp.bfloat16).reshape(experts, capacity)
    ret_rows, ret_gate = (
        lax.all_to_all(back_rows, "ep", split_axis=0, concat_axis=0, tiled=True),
        lax.all_to_all(back_gate, "ep", split_axis=0, concat_axis=0, tiled=True),
    )
    flat_rows = ret_rows.reshape(experts * capacity, width)
    route_back = contract_rows(placing, flat_rows)
    moe_grad = jnp.sum(route_back.reshape(tok_rows, topw, width), axis=1).astype(jnp.bfloat16)
    gate_back = jnp.sum(
        placing.astype(jnp.float32) * ret_gate.reshape(experts * capacity, 1).astype(jnp.float32),
        axis=0,
    )
    gate_grad = gate_back.reshape(tok_rows, topw).astype(jnp.bfloat16)
    return (moe_grad, gate_grad, grad_w_gate, grad_w_up, grad_w_down)


def body(*args):
    moe_grad, gate_row, overflow, grad_gate, grad_up, grad_down, _, _ = fast(*args)
    made = (moe_grad, gate_row.reshape(-1, 1), grad_gate, grad_up, grad_down)
    return lax.cond(overflow[0, 0] > 0.0, lambda: general(*args), lambda: made)


def solution(mesh):
    rows = P(("ep", "fsdp"), None)
    columns = P("ep", None, "fsdp")
    return jax.shard_map(
        body,
        mesh=mesh,
        in_specs=(rows, rows, rows, rows, columns, columns, P("ep", "fsdp", None)),
        out_specs=(rows, rows, columns, columns, P("ep", "fsdp", None)),
        check_vma=False,
    )
```

```python
import functools
import math

import jax
import jax.numpy as jnp
from jax import lax
from jax.experimental import pallas as pl
from jax.experimental.pallas import tpu as pltpu
from jax.sharding import PartitionSpec as P

BF = jnp.bfloat16
F32 = jnp.float32
CAP = 7
UNIT = 16
FLAG_ROW = 2 * CAP
STEPS = 4
BLOCKS = 8
SLOTS = BLOCKS * UNIT
LIST = 80
ROWS = 4 * LIST
PADDED = 384
LANES = 128
OVER_Z = (0, 1)
MESH = pl.DeviceIdType.MESH


def nn(left, right):
    return jnp.dot(left, right, preferred_element_type=F32)


def nt(left, right):
    return lax.dot_general(left, right, (((1,), (1,)), ((), ())), preferred_element_type=F32)


def tn(left, right):
    return lax.dot_general(left, right, (((0,), (0,)), ((), ())), preferred_element_type=F32)


def iota(shape, dim):
    return lax.broadcasted_iota(jnp.int32, shape, dim)


def ones(where):
    return where.astype(F32).astype(BF)


def kernel(
    moe_input, out_grad, ids, gates, w_gate_hbm, w_up_hbm, w_down_hbm,
    moe_grad, gate_grad, overflow, grad_gate_hbm, grad_up_hbm, grad_down_hbm, lists_hbm, returned_hbm,
    w_gate, w_up, w_down, units, relay, arrived, all_dense, lists, picks, all_part, twin_out, twin_in, z_in, all_far, all_near, back,
    acc, packed, turned, flag_out, flag_in,
    w_sem, y_send, y_recv, unit_send, unit_recv, own_send, own_recv, fwd_send, fwd_recv, twin_send, twin_recv,
    part_send, part_recv, z_send, z_recv, far_send, far_recv, near_send, near_recv,
    part_free, z_free, far_free, near_free,
    back_send, back_recv, flag_send, flag_recv, pull_sem, out_sem,
):
    tokens, width = moe_input.shape
    hid = w_gate.shape[1]
    half = width // 2
    full = half + LANES
    ep = lax.axis_index("ep")
    fs = lax.axis_index("fsdp")
    z = lax.rem(fs, 2) * 2 + ep // 8
    y = lax.rem(ep // 2, 4)
    core = lax.rem(ep, 2)
    x = fs // 2
    mine = z * 2 + core
    other = 1 - core

    def at(ax, ay, az, ac):
        return (lax.rem(az, 2) * 8 + ay * 2 + ac, ax * 2 + az // 2)

    def shift(v, n):
        return lax.rem(v + n, 4)

    plus = at(shift(x, 1), y, z, core)
    minus = at(shift(x, 3), y, z, core)
    twin = at(x, y, z, other)
    high = z // 2
    far_z = at(x, y, shift(z, 2), core)
    keep = (full // LANES + 1) // 2 * LANES
    kept_cols = pl.ds(pl.multiple_of(high * (full - keep), LANES), keep)
    sent_cols = pl.ds(pl.multiple_of((1 - high) * (full - keep), LANES), keep)
    remote = functools.partial(pltpu.make_async_remote_copy, device_id_type=MESH)
    offsets = [(dy, dz, dc) for dy in range(4) for dz in range(4) for dc in range(2)]

    def plane(dy, dz, dc):
        return shift(y, dy), shift(z, dz), lax.rem(core + dc, 2)

    weights = [
        pltpu.make_async_copy(w_gate_hbm.at[0], w_gate, w_sem.at[0]),
        pltpu.make_async_copy(w_up_hbm.at[0], w_up, w_sem.at[1]),
        pltpu.make_async_copy(w_down_hbm.at[0], w_down, w_sem.at[2]),
    ]
    for copy in weights:
        copy.start()
    barrier = pltpu.get_barrier_semaphore()
    partners = [plus, minus] + [at(x, *plane(*o)) for o in offsets[1:]]
    for partner in partners:
        pl.semaphore_signal(barrier, 1, device_id=partner, device_id_type=MESH)

    token_square = (tokens, tokens)
    diagonal = iota(token_square, 0) == iota(token_square, 1)

    def upright(row):
        return jnp.sum(jnp.where(diagonal, row, 0.0), axis=1, keepdims=True)

    row_id = ids[...]
    col_id = upright(row_id.astype(F32)).astype(jnp.int32)
    same = col_id == row_id
    above = iota((tokens, tokens), 0) < iota((tokens, tokens), 1)
    below = iota((tokens, tokens), 0) > iota((tokens, tokens), 1)
    slot_row = jnp.sum((same & above).astype(F32), axis=0, keepdims=True).astype(jnp.int32)
    slot_col = jnp.sum((same & below).astype(F32), axis=1, keepdims=True).astype(jnp.int32)
    target = ((row_id // 2) % 4 * 2 + row_id // 8) * UNIT + (row_id % 2) * CAP + slot_row
    place = (iota((SLOTS, tokens), 0) == target).astype(F32)
    taken = jnp.sum(place, axis=1, keepdims=True)
    place = place.astype(BF)
    square = (SLOTS, SLOTS)
    spread = ones(iota(square, 1) == mine * UNIT + iota(square, 0) % UNIT)
    to_flag = ones(
        (iota(square, 0) % UNIT == FLAG_ROW) & (iota(square, 0) // UNIT == iota(square, 1) // UNIT)
    )
    flags = nn(to_flag, (taken * spread.astype(F32)).astype(BF))
    gate = upright(gates[...].astype(F32))
    step = 1024

    def pack(i, carry):
        cols = pl.ds(pl.multiple_of(i * step, step), step)
        gated = (gate * out_grad[:, cols].astype(F32)).astype(BF)
        units[:, 0, :, :, cols] = nn(place, moe_input[:, cols]).astype(BF).reshape(4, 2, UNIT, step)
        units[:, 1, :, :, cols] = nn(place, gated).astype(BF).reshape(4, 2, UNIT, step)
        return carry

    lax.fori_loop(0, width // step, pack, 0)
    for a in range(2):
        head = units[:, a, :, :, 0:LANES].reshape(SLOTS, LANES).astype(F32)
        units[:, a, :, :, 0:LANES] = (head + flags).astype(BF).reshape(4, 2, UNIT, LANES)
    from_pair = iota((tokens, 2 * SLOTS), 1)
    token_map = ones(
        (from_pair // 64 == (col_id // 2) % 4)
        & ((from_pair // UNIT) % 2 == col_id // 8)
        & (from_pair % UNIT == (col_id % 2) * CAP + slot_col)
    )
    pl.semaphore_wait(barrier, len(partners))

    unit_copies = []

    over_y = {}

    def units_over(k):
        ay = shift(y, 4 - k)
        over_y[k] = remote(units.at[ay], relay.at[k - 1], y_send.at[k], y_recv.at[k], device_id=at(x, ay, z, core))
        over_y[k].start()
        unit_copies.append(over_y[k])

    def units_out(k):
        if k:
            over_y[k].wait_recv()
        for dz in range(4):
            for dc in range(2):
                _, az, ac = plane(0, dz, dc)
                low = lax.rem(az, 2)
                src = relay.at[k - 1, ac, low] if k else units.at[y, ac, low]
                dst = arrived.at[k * BLOCKS + mine]
                index = (k * 4 + dz) * 2 + dc
                sem = unit_recv.at[k * BLOCKS + mine]
                if dz or dc:
                    copy = remote(src, dst, unit_send.at[index], sem, device_id=at(x, y, az, ac))
                    copy.start()
                    unit_copies.append(copy)
                else:
                    pltpu.make_async_copy(src, dst, sem).start()

    earlier = ones(iota(square, 0) < iota(square, 1))
    owner = iota(square, 0) % UNIT
    lane = iota(square, 1)
    whose = ones(((lane == 0) & (owner < CAP)) | ((lane == 1) & (owner >= CAP) & (owner < 2 * CAP)))
    own, kept, fwd, twins, parts, zs, far, near, backs = ({} for _ in range(9))
    over = [jnp.zeros((1, 1), F32)]

    def take_in(k):
        for b in range(BLOCKS):
            j = k * BLOCKS + b
            pltpu.make_async_copy(arrived.at[j], arrived.at[j], unit_recv.at[j]).wait()
        dense = all_dense.at[k % 2]
        if k >= 2:
            for copy in own[k - 2] + twins[k - 2][:1]:
                copy.wait_send()
            kept[k - 2].wait()
        tiles = arrived[k * BLOCKS : (k + 1) * BLOCKS, :, 0:LANES].astype(F32)
        flag = jnp.where(iota(tiles.shape, 1) == FLAG_ROW, tiles, 0.0)
        flag = jnp.sum(flag.reshape(SLOTS, LANES), axis=0, keepdims=True)
        rank = nn(flag.astype(BF), earlier)
        count = jnp.sum(flag, axis=1, keepdims=True)
        over[0] = jnp.maximum(over[0], (count > LIST).astype(F32))
        pick = ones((iota((LIST, SLOTS), 0).astype(F32) == rank) & (flag > 0.5))
        picks[k] = pick
        masks = nn(pick, whose) + jnp.where(iota((LIST, LANES), 1) == 2, over[0], 0.0)
        dense[:, width : width + LANES] = masks.astype(BF)

        def move(i, carry):
            cols = pl.ds(pl.multiple_of(i * step, step), step)
            found = arrived[k * BLOCKS : (k + 1) * BLOCKS, :, cols].reshape(SLOTS, step)
            dense[:, cols] = nn(pick, found).astype(BF)
            return carry

        lax.fori_loop(0, width // step, move, 0)
        to = lists_hbm.at[core, k]
        own[k] = [
            remote(dense, to.at[1], own_send.at[k, 0], own_recv.at[k, 0], device_id=plus),
            remote(dense, to.at[2], own_send.at[k, 1], own_recv.at[k, 1], device_id=minus),
        ]
        twins[k] = [remote(dense, to.at[0], twin_send.at[k, 0], twin_recv.at[k, 0], device_id=twin)]
        kept[k] = pltpu.make_async_copy(dense, to.at[0], own_send.at[k, 2])
        for copy in own[k] + twins[k] + [kept[k]]:
            copy.start()

    def forward(k):
        to = lists_hbm.at[core, k]
        cut = 48 if k % 2 == 0 else 32
        low, high = pl.ds(0, cut), pl.ds(cut, LIST - cut)
        fwd[k] = [
            remote(to.at[1, low], to.at[3, low], fwd_send.at[k, 0], fwd_recv.at[k, 0], device_id=plus),
            remote(to.at[2, high], to.at[3, high], fwd_send.at[k, 1], fwd_recv.at[k, 1], device_id=minus),
        ]
        for i in range(2):
            own[k][i].wait_recv()
            fwd[k][i].start()
            copy = remote(to.at[i + 1], to.at[i + 1], twin_send.at[k, i + 1], twin_recv.at[k, i + 1], device_id=twin)
            copy.start()
            twins[k].append(copy)

    def share(k):
        to = lists_hbm.at[core, k]
        for copy in fwd[k]:
            copy.wait_recv()
        copy = remote(to.at[3], to.at[3], twin_send.at[k, 3], twin_recv.at[k, 3], device_id=twin)
        copy.start()
        twins[k].append(copy)

    def compute(k):
        if k >= 2:
            kept[k].wait()
        for copy in twins[k]:
            copy.wait_recv()
        pull = pltpu.make_async_copy(lists_hbm.at[:, k], lists, pull_sem.at[0])
        pull.start()
        acc[...] = jnp.zeros_like(acc)
        pull.wait()

        def gather(i, carry):
            cols = pl.ds(pl.multiple_of(i * step, step), step)
            left = lists[0, :, :, cols].reshape(ROWS, step)
            acc[0:ROWS, 0:hid] += nn(left, w_gate[cols, :])
            acc[0:ROWS, hid : 2 * hid] += nn(left, w_up[cols, :])
            acc[0:ROWS, 2 * hid : 3 * hid] += nt(lists[1, :, :, cols].reshape(ROWS, step), w_down[:, cols])
            return carry

        lax.fori_loop(0, width // step, gather, 0)
        part = all_part.at[k % 3]
        if k:
            parts[k - 1].wait_send()
        if k >= 3:
            for copy in far[k - 3] + near[k - 3]:
                copy.wait_send()
        for r in range(4):
            rows = slice(r * LIST, (r + 1) * LIST)
            tile = lists[0, r, :, width : width + LANES].astype(F32)
            mask = jnp.sum(jnp.where(iota(tile.shape, 1) == core, tile, 0.0), axis=1, keepdims=True)
            pre_gate = acc[rows, 0:hid]
            pre_up = acc[rows, hid : 2 * hid]
            scaled = acc[rows, 2 * hid : 3 * hid] * mask
            sig = jax.nn.sigmoid(pre_gate)
            act = pre_gate * sig
            slope = sig * (1.0 + pre_gate * (1.0 - sig))
            hidden = (act * pre_up).astype(BF).astype(F32) * mask
            piece = jnp.sum(hidden * scaled, axis=1, keepdims=True) * (1.0 / math.sqrt(width))
            acc[rows, 0:hid] = scaled * pre_up * slope
            acc[rows, hid : 2 * hid] = scaled * act
            acc[rows, 2 * hid : 3 * hid] = hidden
            wide = jnp.broadcast_to(piece, (LIST, LANES)).astype(BF)
            part[r, :, half:full] = wide
            twin_out[r, :, half:full] = wide
        turned[k] = jnp.transpose(acc[...]).astype(BF)
        packed[...] = acc[0:ROWS, 0 : 2 * hid].astype(BF)
        span = 512

        def rows_back(into, first):
            def one(i, carry):
                cols = pl.ds(pl.multiple_of(i * span, span), span)
                here = pl.ds(pl.multiple_of(first + i * span, span), span)
                total = nt(packed[:, 0:hid], w_gate[here, :]) + nt(packed[:, hid : 2 * hid], w_up[here, :])
                into[:, :, cols] = total.astype(BF).reshape(4, LIST, span)
                return carry

            lax.fori_loop(0, half // span, one, 0)

        rows_back(twin_out, other * half)
        if k:
            pl.semaphore_wait(part_free, 1)
        parts[k] = remote(twin_out, twin_in, part_send.at[k], part_recv.at[k], device_id=twin)
        parts[k].start()
        rows_back(part, core * half)

    def window(k):
        return (kept_cols, pl.ds(0, keep)) if k in OVER_Z else (pl.ds(0, full), pl.ds(0, full))

    def start_far(k):
        part = all_part.at[k % 3]
        far_in = all_far.at[k % 2]
        here, there = window(k)
        cut = 48 if k % 2 == 0 else 32
        low, up = pl.ds(0, cut), pl.ds(cut, LIST - cut)
        if k >= 2:
            pl.semaphore_wait(far_free.at[k % 2], 2)
        far[k] = [
            remote(part.at[3, low, here], far_in.at[0, low, there], far_send.at[k, 0], far_recv.at[k, 0], device_id=plus),
            remote(part.at[3, up, here], far_in.at[1, up, there], far_send.at[k, 1], far_recv.at[k, 1], device_id=minus),
        ]
        for copy in far[k]:
            copy.start()

    def merge(k):
        part = all_part.at[k % 3]
        parts[k].wait_recv()

        def add(r, carry):
            part[r] = (part[r].astype(F32) + twin_in[r].astype(F32)).astype(BF)
            return carry

        if k in OVER_Z:
            lax.fori_loop(0, 4, add, 0)
            if k != OVER_Z[0]:
                pl.semaphore_wait(z_free, 1)
            zs[k] = remote(part.at[:, :, sent_cols], z_in, z_send.at[k], z_recv.at[k], device_id=far_z)
            zs[k].start()
        else:
            add(3, 0)
            start_far(k)
            lax.fori_loop(0, 3, add, 0)
        if k < STEPS - 1:
            pl.semaphore_signal(part_free, 1, device_id=twin, device_id_type=MESH)

    def add_z(k):
        part = all_part.at[k % 3]
        zs[k].wait()

        def add(r, carry):
            part[r, :, kept_cols] = (part[r, :, kept_cols].astype(F32) + z_in[r].astype(F32)).astype(BF)
            return carry

        lax.fori_loop(0, 4, add, 0)
        if k != OVER_Z[-1]:
            pl.semaphore_signal(z_free, 1, device_id=far_z, device_id_type=MESH)
        start_far(k)

    def pass_on(k):
        part = all_part.at[k % 3]
        far_in, near_in = all_far.at[k % 2], all_near.at[k % 2]
        here, there = window(k)
        if k >= 2:
            pl.semaphore_wait(near_free.at[k % 2], 2)
        near[k] = [
            remote(part.at[2, :, here], near_in.at[0, :, there], near_send.at[k, 0], near_recv.at[k, 0], device_id=plus),
            remote(part.at[1, :, here], near_in.at[1, :, there], near_send.at[k, 1], near_recv.at[k, 1], device_id=minus),
        ]
        cut = 48 if k % 2 == 0 else 32
        for i, rel, rows, giver in ((0, 2, slice(0, cut), minus), (1, 1, slice(cut, LIST), plus)):
            far[k][i].wait_recv()
            part[rel, rows, here] = (part[rel, rows, here].astype(F32) + far_in[i, rows, there].astype(F32)).astype(BF)
            if k < STEPS - 2:
                pl.semaphore_signal(far_free.at[k % 2], 1, device_id=giver, device_id_type=MESH)
            near[k][i].start()

    def send_back(k):
        part = all_part.at[k % 3]
        near_in = all_near.at[k % 2]
        for copy in near[k]:
            copy.wait_recv()
        slot = k % 2
        if k >= 2:
            for copy in backs[k - 2]:
                copy.wait_send()
        if k in OVER_Z:
            back[slot] = jnp.zeros(back.shape[1:], BF)
            span = keep // 3
            for first in range(0, keep, span):
                there = pl.ds(pl.multiple_of(high * (full - keep) + first, LANES), span)
                total = tn(picks[k], part[0, :, there]) + tn(picks[k], near_in[0, :, first : first + span])
                total = total + tn(picks[k], near_in[1, :, first : first + span])
                if first == 0:
                    twice = (iota(total.shape, 1) < 2 * keep - full) & (high == 1)
                    total = jnp.where(twice, 0.0, total)
                back[slot, :, :, there] = total.astype(BF).reshape(BLOCKS, UNIT, span)
        for first in range(0, 0 if k in OVER_Z else full, 1024):
            cols = slice(first, min(first + 1024, full))
            total = tn(picks[k], part[0, :, cols]) + tn(picks[k], near_in[0, :, cols])
            total = total + tn(picks[k], near_in[1, :, cols])
            back[slot, :, :, cols] = total.astype(BF).reshape(BLOCKS, UNIT, cols.stop - cols.start)
        if k < STEPS - 2:
            for giver in (minus, plus):
                pl.semaphore_signal(near_free.at[k % 2], 1, device_id=giver, device_id_type=MESH)
        me = core * 16 + y * 4 + z
        backs[k] = []
        for dz in range(4):
            for dc in range(2):
                ay, az, ac = plane(k, dz, dc)
                src = back.at[slot, az * 2 + ac]
                index = (k * 4 + dz) * 2 + dc
                if k or dz or dc:
                    copy = remote(src, returned_hbm.at[me], back_send.at[index], back_recv.at[me], device_id=at(x, ay, az, ac))
                    copy.start()
                    backs[k].append(copy)
                else:
                    stay = pltpu.make_async_copy(src, returned_hbm.at[me], pull_sem.at[1])
                    stay.start()
                    stay.wait()

    flag_copies = []

    def tell():
        tile = jnp.maximum(lists[0, 0, 0:16, width : width + LANES], lists[0, 1, 0:16, width : width + LANES])
        tile = jnp.maximum(tile, lists[0, 2, 0:16, width : width + LANES])
        tile = jnp.maximum(tile, lists[0, 3, 0:16, width : width + LANES]).astype(F32)
        flag_out[...] = jnp.where(iota(tile.shape, 1) == 2, tile, 0.0).astype(BF)
        me = y * BLOCKS + mine
        for i, o in enumerate(offsets):
            if i:
                copy = remote(flag_out, flag_in.at[me], flag_send.at[i], flag_recv.at[me], device_id=at(x, *plane(*o)))
                copy.start()
                flag_copies.append(copy)
        flag_in[me] = flag_out[...]

    scale = 1.0 / math.sqrt(tokens * 8)
    span = 512
    blocks = width // span
    out_copies = []

    def stream(i, slot):
        cols = pl.ds(pl.multiple_of(i * span, span), span)
        made = []
        for k in range(STEPS):
            there = pl.ds(pl.multiple_of((slot * STEPS + k) * span, span), span)
            made.append(
                pltpu.make_async_copy(
                    lists_hbm.at[:, k, :, :, cols], lists.at[:, :, :, there], out_sem.at[slot * STEPS + k]
                )
            )
        return made

    def gradients(first, last):
        def one(i, carry):
            slot = lax.rem(i, 2)
            cols = pl.ds(pl.multiple_of(i * span, span), span)

            @pl.when(i + 1 < blocks)
            def _():
                for copy in stream(i + 1, 1 - slot):
                    copy.start()

            for copy in stream(i, slot):
                copy.wait()
            total = jnp.zeros((2 * hid, span), F32)
            down = jnp.zeros((hid, span), F32)
            for k in range(STEPS):
                there = pl.ds(pl.multiple_of((slot * STEPS + k) * span, span), span)
                total = total + nn(turned[k, 0 : 2 * hid, 0:ROWS], lists[0, :, :, there].reshape(ROWS, span))
                down = down + nn(turned[k, 2 * hid : 3 * hid, 0:ROWS], lists[1, :, :, there].reshape(ROWS, span))
            total = total * scale
            w_gate[cols, :] = jnp.transpose(total[0:hid]).astype(BF)
            w_up[cols, :] = jnp.transpose(total[hid : 2 * hid]).astype(BF)
            w_down[:, cols] = (down * scale).astype(BF)
            return carry

        if first == 0:
            for copy in stream(0, 0):
                copy.start()
        lax.fori_loop(first, last, one, 0)
        rows = pl.ds(first * span, (last - first) * span)
        n = 8 + len(out_copies)
        made = [
            pltpu.make_async_copy(w_gate.at[rows], grad_gate_hbm.at[0, rows], out_sem.at[n]),
            pltpu.make_async_copy(w_up.at[rows], grad_up_hbm.at[0, rows], out_sem.at[n + 1]),
            pltpu.make_async_copy(w_down.at[:, rows], grad_down_hbm.at[0, :, rows], out_sem.at[n + 2]),
        ]
        for copy in made:
            copy.start()
        out_copies.extend(made)

    units_out(0)
    for k in range(1, STEPS):
        units_over(k)
    take_in(0)
    units_out(1)
    take_in(1)
    units_out(2)
    forward(0)
    take_in(2)
    units_out(3)
    forward(1)
    share(0)
    take_in(3)
    for copy in weights:
        copy.wait()
    compute(0)
    merge(0)
    share(1)
    forward(2)
    compute(1)
    add_z(0)
    merge(1)
    share(2)
    forward(3)
    compute(2)
    pass_on(0)
    add_z(1)
    merge(2)
    share(3)
    send_back(0)
    pass_on(1)
    compute(3)
    tell()
    pass_on(2)
    merge(3)
    send_back(1)
    gradients(0, 2)
    send_back(2)
    pass_on(3)
    gradients(2, 7)
    send_back(3)
    gradients(7, 14)

    for dy, dz, dc in offsets[1:]:
        ay, az, ac = plane(dy, dz, dc)
        j = ac * 16 + ay * 4 + az
        pltpu.make_async_copy(back.at[0, 0], returned_hbm.at[j], back_recv.at[j]).wait()
        j = ay * BLOCKS + az * 2 + ac
        pltpu.make_async_copy(flag_out, flag_in.at[j], flag_recv.at[j]).wait()
    pull = pltpu.make_async_copy(returned_hbm, arrived.at[:, :, pl.ds(0, full)], pull_sem.at[0])
    pull.start()
    seen = jnp.max(flag_in[...].astype(F32).reshape(32 * 16, LANES), axis=0, keepdims=True)
    overflow[...] = jnp.broadcast_to(jnp.max(seen, axis=1, keepdims=True), overflow.shape)
    pull.wait()
    for h in range(2):
        for first in range(0, half, 512):
            found = arrived[h * 16 : (h + 1) * 16, :, first : first + 512].reshape(2 * SLOTS, 512)
            moe_grad[:, h * half + first : h * half + first + 512] = nn(token_map, found).astype(BF)
    found = arrived[0:16, :, half:full].reshape(2 * SLOTS, LANES)
    sums = nn(token_map, found)[:, 0:1] / gate
    gate_grad[...] = jnp.sum(jnp.where(diagonal, sums, 0.0), axis=0, keepdims=True).astype(BF)

    for copy in out_copies:
        copy.wait()
    for copy in unit_copies + flag_copies + [parts[STEPS - 1]]:
        copy.wait_send()
    for k in range(STEPS):
        done = fwd[k] + twins[k][1:] if k < 2 else own[k] + fwd[k] + twins[k]
        for copy in done:
            copy.wait_send()
    for k in range(STEPS - 3, STEPS):
        for copy in far[k] + near[k]:
            copy.wait_send()
    for copy in backs[STEPS - 2] + backs[STEPS - 1]:
        copy.wait_send()


def fast(moe_input, out_grad, expert_ids, gate_values, w_gate, w_up, w_down):
    tokens, width = moe_input.shape
    hid = w_gate.shape[2]
    full = width // 2 + LANES
    keep = (full // LANES + 1) // 2 * LANES
    vmem = pl.BlockSpec(memory_space=pltpu.VMEM)
    anywhere = pl.BlockSpec(memory_space=pl.ANY)
    dma = pltpu.SemaphoreType.DMA
    regular = pltpu.SemaphoreType.REGULAR
    return pl.pallas_call(
        kernel,
        out_shape=[
            jax.ShapeDtypeStruct((tokens, width), BF),
            jax.ShapeDtypeStruct((1, tokens), BF),
            jax.ShapeDtypeStruct((8, LANES), F32),
            jax.ShapeDtypeStruct(w_gate.shape, BF),
            jax.ShapeDtypeStruct(w_up.shape, BF),
            jax.ShapeDtypeStruct(w_down.shape, BF),
            jax.ShapeDtypeStruct((2, STEPS, 4, LIST, width + LANES), BF),
            jax.ShapeDtypeStruct((32, UNIT, full), BF),
        ],
        in_specs=[vmem] * 4 + [anywhere] * 3,
        out_specs=[vmem] * 3 + [anywhere] * 5,
        scratch_shapes=[
            pltpu.VMEM((width, hid), BF),
            pltpu.VMEM((width, hid), BF),
            pltpu.VMEM((hid, width), BF),
            pltpu.VMEM((4, 2, 2, UNIT, width), BF),
            pltpu.VMEM((STEPS - 1, 2, 2, UNIT, width), BF),
            pltpu.VMEM((STEPS * BLOCKS, UNIT, width), BF),
            pltpu.VMEM((2, LIST, width + LANES), BF),
            pltpu.VMEM((2, 4, LIST, width + LANES), BF),
            pltpu.VMEM((STEPS, LIST, SLOTS), BF),
            pltpu.VMEM((3, 4, LIST, full), BF),
            pltpu.VMEM((4, LIST, full), BF),
            pltpu.VMEM((4, LIST, full), BF),
            pltpu.VMEM((4, LIST, keep), BF),
            pltpu.VMEM((2, 2, LIST, full), BF),
            pltpu.VMEM((2, 2, LIST, full), BF),
            pltpu.VMEM((2, BLOCKS, UNIT, full), BF),
            pltpu.VMEM((PADDED, 3 * hid), F32),
            pltpu.VMEM((ROWS, 2 * hid), BF),
            pltpu.VMEM((STEPS, 3 * hid, PADDED), BF),
            pltpu.VMEM((16, LANES), BF),
            pltpu.VMEM((32, 16, LANES), BF),
            dma((3,)),
            dma((STEPS,)),
            dma((STEPS,)),
            dma((32,)),
            dma((32,)),
            dma((STEPS, 3)),
            dma((STEPS, 2)),
            dma((STEPS, 2)),
            dma((STEPS, 2)),
            dma((STEPS, 4)),
            dma((STEPS, 4)),
            dma((STEPS,)),
            dma((STEPS,)),
            dma((STEPS,)),
            dma((STEPS,)),
            dma((STEPS, 2)),
            dma((STEPS, 2)),
            dma((STEPS, 2)),
            dma((STEPS, 2)),
            regular,
            regular,
            pltpu.SemaphoreType.REGULAR((2,)),
            pltpu.SemaphoreType.REGULAR((2,)),
            dma((32,)),
            dma((32,)),
            dma((32,)),
            dma((32,)),
            dma((2,)),
            dma((17,)),
        ],
        compiler_params=pltpu.CompilerParams(
            collective_id=0, has_side_effects=True, vmem_limit_bytes=63 * 2**20
        ),
    )(moe_input, out_grad, expert_ids.reshape(1, tokens), gate_values.reshape(1, tokens), w_gate, w_up, w_down)


def silu_parts(value):
    sig = jax.nn.sigmoid(value)
    return (value * sig, sig * (1.0 + value * (1.0 - sig)))


def contract_rows(left, right):
    return lax.dot_general(
        left, right, (((0,), (0,)), ((), ())), preferred_element_type=jnp.float32
    )


def contract_cols(left, right):
    return lax.dot_general(
        left, right, (((1,), (1,)), ((), ())), preferred_element_type=jnp.float32
    )


def general(moe_input, out_grad, expert_ids, gate_values, w_gate, w_up, w_down):
    tok_rows = moe_input.shape[0]
    width = moe_input.shape[1]
    topw = expert_ids.shape[1]
    experts = lax.axis_size("ep")
    groups = lax.axis_size("fsdp")
    capacity = (3 * tok_rows * topw + experts - 1) // experts
    routes = tok_rows * topw
    flat_ids = expert_ids.reshape(routes)
    onehot = (flat_ids[:, None] == jnp.arange(experts, dtype=jnp.int32)[None, :]).astype(jnp.int32)
    earlier = jnp.cumsum(onehot, axis=0) - onehot
    slot_index = jnp.sum(earlier * onehot, axis=1)
    target = flat_ids * capacity + slot_index
    placing = (jnp.arange(experts * capacity, dtype=jnp.int32)[:, None] == target[None, :]).astype(
        jnp.bfloat16
    )
    route_input = jnp.repeat(moe_input, topw, axis=0)
    route_grad = jnp.repeat(out_grad, topw, axis=0)
    send_input = (
        jnp.dot(placing, route_input, preferred_element_type=jnp.float32)
        .astype(jnp.bfloat16)
        .reshape(experts, capacity, width)
    )
    send_grad = (
        jnp.dot(placing, route_grad, preferred_element_type=jnp.float32)
        .astype(jnp.bfloat16)
        .reshape(experts, capacity, width)
    )
    send_gate = jnp.sum(
        placing.astype(jnp.float32) * gate_values.reshape(1, routes).astype(jnp.float32), axis=1
    )
    send_gate = send_gate.astype(jnp.bfloat16).reshape(experts, capacity)
    recv_input, recv_grad, recv_gate = (
        lax.all_to_all(send_input, "ep", split_axis=0, concat_axis=0, tiled=True),
        lax.all_to_all(send_grad, "ep", split_axis=0, concat_axis=0, tiled=True),
        lax.all_to_all(send_gate, "ep", split_axis=0, concat_axis=0, tiled=True),
    )
    weight_gate = w_gate[0]
    weight_up = w_up[0]
    weight_down = w_down[0]
    expert_scale = 1.0 / math.sqrt(tok_rows * groups)
    gate_scale = 1.0 / math.sqrt(width)

    def gathered(own):
        copies = jnp.broadcast_to(own[None], (groups,) + own.shape)
        copies = lax.all_to_all(copies, "fsdp", split_axis=0, concat_axis=0, tiled=True)
        return copies.reshape((groups * own.shape[0],) + own.shape[1:])

    def summed(pieces):
        spread = lax.all_to_all(pieces, "fsdp", split_axis=0, concat_axis=0, tiled=True)
        spread = spread.reshape((groups, pieces.shape[0] // groups) + pieces.shape[1:])
        return jnp.sum(spread.astype(jnp.float32), axis=0)

    piece_input = gathered(recv_input)
    piece_grad = gathered(recv_grad)
    piece_gate = gathered(recv_gate)
    count = piece_input.shape[0] * piece_input.shape[1]
    rows_in = piece_input.reshape(count, width)
    rows_grad = piece_grad.reshape(count, width)
    gates = piece_gate.reshape(count, 1).astype(jnp.float32)
    pre_gate = jnp.dot(rows_in, weight_gate, preferred_element_type=jnp.float32)
    pre_up = jnp.dot(rows_in, weight_up, preferred_element_type=jnp.float32)
    act, slope = silu_parts(pre_gate)
    hidden = (act * pre_up).astype(jnp.bfloat16)
    raw = contract_cols(rows_grad, weight_down)
    scaled = gates * raw
    grad_pre_gate = (scaled * pre_up * slope).astype(jnp.bfloat16)
    grad_pre_up = (scaled * act).astype(jnp.bfloat16)
    gated_grad = (gates * rows_grad.astype(jnp.float32)).astype(jnp.bfloat16)
    acc_gate = contract_rows(rows_in, grad_pre_gate)
    acc_up = contract_rows(rows_in, grad_pre_up)
    acc_down = contract_rows(hidden, gated_grad)
    rows_back = contract_cols(grad_pre_gate, weight_gate) + contract_cols(grad_pre_up, weight_up)
    gate_back = jnp.sum(hidden.astype(jnp.float32) * raw, axis=1) * gate_scale
    part_rows = rows_back
    part_gate = gate_back
    acc_gate, acc_up, acc_down, part_rows, part_gate = (
        acc_gate,
        acc_up,
        acc_down,
        part_rows,
        part_gate,
    )
    grad_w_gate = (acc_gate * expert_scale).astype(jnp.bfloat16)[None]
    grad_w_up = (acc_up * expert_scale).astype(jnp.bfloat16)[None]
    grad_w_down = (acc_down * expert_scale).astype(jnp.bfloat16)[None]
    summed_rows = summed(part_rows.astype(jnp.bfloat16))
    summed_gate = summed(part_gate.astype(jnp.bfloat16))
    back_rows = summed_rows.astype(jnp.bfloat16).reshape(experts, capacity, width)
    back_gate = summed_gate.astype(jnp.bfloat16).reshape(experts, capacity)
    ret_rows, ret_gate = (
        lax.all_to_all(back_rows, "ep", split_axis=0, concat_axis=0, tiled=True),
        lax.all_to_all(back_gate, "ep", split_axis=0, concat_axis=0, tiled=True),
    )
    flat_rows = ret_rows.reshape(experts * capacity, width)
    route_back = contract_rows(placing, flat_rows)
    moe_grad = jnp.sum(route_back.reshape(tok_rows, topw, width), axis=1).astype(jnp.bfloat16)
    gate_back = jnp.sum(
        placing.astype(jnp.float32) * ret_gate.reshape(experts * capacity, 1).astype(jnp.float32),
        axis=0,
    )
    gate_grad = gate_back.reshape(tok_rows, topw).astype(jnp.bfloat16)
    return (moe_grad, gate_grad, grad_w_gate, grad_w_up, grad_w_down)


def body(*args):
    moe_grad, gate_row, overflow, grad_gate, grad_up, grad_down, _, _ = fast(*args)
    made = (moe_grad, gate_row.reshape(-1, 1), grad_gate, grad_up, grad_down)
    return lax.cond(overflow[0, 0] > 0.0, lambda: general(*args), lambda: made)


def solution(mesh):
    rows = P(("ep", "fsdp"), None)
    columns = P("ep", None, "fsdp")
    return jax.shard_map(
        body,
        mesh=mesh,
        in_specs=(rows, rows, rows, rows, columns, columns, P("ep", "fsdp", None)),
        out_specs=(rows, rows, columns, columns, P("ep", "fsdp", None)),
        check_vma=False,
    )
```

```python
import functools
import math

import jax
import jax.numpy as jnp
from jax import lax
from jax.experimental import pallas as pl
from jax.experimental.pallas import tpu as pltpu
from jax.sharding import PartitionSpec as P

BF = jnp.bfloat16
F32 = jnp.float32
CAP = 7
UNIT = 16
FLAG_ROW = 2 * CAP
STEPS = 4
BLOCKS = 8
SLOTS = BLOCKS * UNIT
LIST = 80
ROWS = 4 * LIST
PADDED = 384
LANES = 128
OVER_Z = (0, 1)
MESH = pl.DeviceIdType.MESH


def nn(left, right):
    return jnp.dot(left, right, preferred_element_type=F32)


def nt(left, right):
    return lax.dot_general(left, right, (((1,), (1,)), ((), ())), preferred_element_type=F32)


def tn(left, right):
    return lax.dot_general(left, right, (((0,), (0,)), ((), ())), preferred_element_type=F32)


def iota(shape, dim):
    return lax.broadcasted_iota(jnp.int32, shape, dim)


def ones(where):
    return where.astype(F32).astype(BF)


def kernel(
    moe_input, out_grad, ids, gates, w_gate_hbm, w_up_hbm, w_down_hbm,
    moe_grad, gate_grad, overflow, grad_gate_hbm, grad_up_hbm, grad_down_hbm, lists_hbm, returned_hbm,
    w_gate, w_up, w_down, units, relay, arrived, all_dense, lists, picks, all_part, twin_out, twin_in, z_in, all_far, all_near, back,
    acc, packed, turned, flag_out, flag_in,
    w_sem, y_send, y_recv, unit_send, unit_recv, own_send, own_recv, fwd_send, fwd_recv, twin_send, twin_recv,
    part_send, part_recv, z_send, z_recv, far_send, far_recv, near_send, near_recv,
    part_free, z_free, far_free, near_free,
    back_send, back_recv, flag_send, flag_recv, pull_sem, out_sem,
):
    tokens, width = moe_input.shape
    hid = w_gate.shape[1]
    half = width // 2
    full = half + LANES
    ep = lax.axis_index("ep")
    fs = lax.axis_index("fsdp")
    z = lax.rem(fs, 2) * 2 + ep // 8
    y = lax.rem(ep // 2, 4)
    core = lax.rem(ep, 2)
    x = fs // 2
    mine = z * 2 + core
    other = 1 - core

    def at(ax, ay, az, ac):
        return (lax.rem(az, 2) * 8 + ay * 2 + ac, ax * 2 + az // 2)

    def shift(v, n):
        return lax.rem(v + n, 4)

    plus = at(shift(x, 1), y, z, core)
    minus = at(shift(x, 3), y, z, core)
    twin = at(x, y, z, other)
    high = z // 2
    far_z = at(x, y, shift(z, 2), core)
    keep = (full // LANES + 1) // 2 * LANES
    kept_cols = pl.ds(pl.multiple_of(high * (full - keep), LANES), keep)
    sent_cols = pl.ds(pl.multiple_of((1 - high) * (full - keep), LANES), keep)
    remote = functools.partial(pltpu.make_async_remote_copy, device_id_type=MESH)
    offsets = [(dy, dz, dc) for dy in range(4) for dz in range(4) for dc in range(2)]

    def plane(dy, dz, dc):
        return shift(y, dy), shift(z, dz), lax.rem(core + dc, 2)

    weights = [
        pltpu.make_async_copy(w_gate_hbm.at[0], w_gate, w_sem.at[0]),
        pltpu.make_async_copy(w_up_hbm.at[0], w_up, w_sem.at[1]),
        pltpu.make_async_copy(w_down_hbm.at[0], w_down, w_sem.at[2]),
    ]
    for copy in weights:
        copy.start()
    barrier = pltpu.get_barrier_semaphore()
    partners = [plus, minus] + [at(x, *plane(*o)) for o in offsets[1:]]
    for partner in partners:
        pl.semaphore_signal(barrier, 1, device_id=partner, device_id_type=MESH)

    token_square = (tokens, tokens)
    diagonal = iota(token_square, 0) == iota(token_square, 1)

    def upright(row):
        return jnp.sum(jnp.where(diagonal, row, 0.0), axis=1, keepdims=True)

    row_id = ids[...]
    col_id = upright(row_id.astype(F32)).astype(jnp.int32)
    same = col_id == row_id
    above = iota((tokens, tokens), 0) < iota((tokens, tokens), 1)
    below = iota((tokens, tokens), 0) > iota((tokens, tokens), 1)
    slot_row = jnp.sum((same & above).astype(F32), axis=0, keepdims=True).astype(jnp.int32)
    slot_col = jnp.sum((same & below).astype(F32), axis=1, keepdims=True).astype(jnp.int32)
    target = ((row_id // 2) % 4 * 2 + row_id // 8) * UNIT + (row_id % 2) * CAP + slot_row
    place = (iota((SLOTS, tokens), 0) == target).astype(F32)
    taken = jnp.sum(place, axis=1, keepdims=True)
    place = place.astype(BF)
    square = (SLOTS, SLOTS)
    spread = ones(iota(square, 1) == mine * UNIT + iota(square, 0) % UNIT)
    to_flag = ones(
        (iota(square, 0) % UNIT == FLAG_ROW) & (iota(square, 0) // UNIT == iota(square, 1) // UNIT)
    )
    flags = nn(to_flag, (taken * spread.astype(F32)).astype(BF))
    gate = upright(gates[...].astype(F32))
    step = 1024

    def pack(i, carry):
        cols = pl.ds(pl.multiple_of(i * step, step), step)
        gated = (gate * out_grad[:, cols].astype(F32)).astype(BF)
        units[:, 0, :, :, cols] = nn(place, moe_input[:, cols]).astype(BF).reshape(4, 2, UNIT, step)
        units[:, 1, :, :, cols] = nn(place, gated).astype(BF).reshape(4, 2, UNIT, step)
        return carry

    lax.fori_loop(0, width // step, pack, 0)
    for a in range(2):
        head = units[:, a, :, :, 0:LANES].reshape(SLOTS, LANES).astype(F32)
        units[:, a, :, :, 0:LANES] = (head + flags).astype(BF).reshape(4, 2, UNIT, LANES)
    from_pair = iota((tokens, 2 * SLOTS), 1)
    token_map = ones(
        (from_pair // 64 == (col_id // 2) % 4)
        & ((from_pair // UNIT) % 2 == col_id // 8)
        & (from_pair % UNIT == (col_id % 2) * CAP + slot_col)
    )
    pl.semaphore_wait(barrier, len(partners))

    unit_copies = []

    over_y = {}

    def units_over(k):
        ay = shift(y, 4 - k)
        over_y[k] = remote(units.at[ay], relay.at[k - 1], y_send.at[k], y_recv.at[k], device_id=at(x, ay, z, core))
        over_y[k].start()
        unit_copies.append(over_y[k])

    def units_out(k):
        if k:
            over_y[k].wait_recv()
        for dz in range(4):
            for dc in range(2):
                _, az, ac = plane(0, dz, dc)
                low = lax.rem(az, 2)
                src = relay.at[k - 1, ac, low] if k else units.at[y, ac, low]
                dst = arrived.at[k * BLOCKS + mine]
                index = (k * 4 + dz) * 2 + dc
                sem = unit_recv.at[k * BLOCKS + mine]
                if dz or dc:
                    copy = remote(src, dst, unit_send.at[index], sem, device_id=at(x, y, az, ac))
                    copy.start()
                    unit_copies.append(copy)
                else:
                    pltpu.make_async_copy(src, dst, sem).start()

    earlier = ones(iota(square, 0) < iota(square, 1))
    owner = iota(square, 0) % UNIT
    lane = iota(square, 1)
    whose = ones(((lane == 0) & (owner < CAP)) | ((lane == 1) & (owner >= CAP) & (owner < 2 * CAP)))
    own, kept, fwd, twins, parts, zs, far, near, backs = ({} for _ in range(9))
    over = [jnp.zeros((1, 1), F32)]

    def take_in(k):
        for b in range(BLOCKS):
            j = k * BLOCKS + b
            pltpu.make_async_copy(arrived.at[j], arrived.at[j], unit_recv.at[j]).wait()
        dense = all_dense.at[k % 2]
        if k >= 2:
            for copy in own[k - 2] + twins[k - 2][:1]:
                copy.wait_send()
            kept[k - 2].wait()
        tiles = arrived[k * BLOCKS : (k + 1) * BLOCKS, :, 0:LANES].astype(F32)
        flag = jnp.where(iota(tiles.shape, 1) == FLAG_ROW, tiles, 0.0)
        flag = jnp.sum(flag.reshape(SLOTS, LANES), axis=0, keepdims=True)
        rank = nn(flag.astype(BF), earlier)
        count = jnp.sum(flag, axis=1, keepdims=True)
        over[0] = jnp.maximum(over[0], (count > LIST).astype(F32))
        pick = ones((iota((LIST, SLOTS), 0).astype(F32) == rank) & (flag > 0.5))
        picks[k] = pick
        masks = nn(pick, whose) + jnp.where(iota((LIST, LANES), 1) == 2, over[0], 0.0)
        dense[:, width : width + LANES] = masks.astype(BF)

        def move(i, carry):
            cols = pl.ds(pl.multiple_of(i * step, step), step)
            found = arrived[k * BLOCKS : (k + 1) * BLOCKS, :, cols].reshape(SLOTS, step)
            dense[:, cols] = nn(pick, found).astype(BF)
            return carry

        lax.fori_loop(0, width // step, move, 0)
        to = lists_hbm.at[core, k]
        own[k] = [
            remote(dense, to.at[1], own_send.at[k, 0], own_recv.at[k, 0], device_id=plus),
            remote(dense, to.at[2], own_send.at[k, 1], own_recv.at[k, 1], device_id=minus),
        ]
        twins[k] = [remote(dense, to.at[0], twin_send.at[k, 0], twin_recv.at[k, 0], device_id=twin)]
        kept[k] = pltpu.make_async_copy(dense, to.at[0], own_send.at[k, 2])
        for copy in own[k] + twins[k] + [kept[k]]:
            copy.start()

    def forward(k):
        to = lists_hbm.at[core, k]
        cut = 48 if k % 2 == 0 else 32
        low, high = pl.ds(0, cut), pl.ds(cut, LIST - cut)
        fwd[k] = [
            remote(to.at[1, low], to.at[3, low], fwd_send.at[k, 0], fwd_recv.at[k, 0], device_id=plus),
            remote(to.at[2, high], to.at[3, high], fwd_send.at[k, 1], fwd_recv.at[k, 1], device_id=minus),
        ]
        for i in range(2):
            own[k][i].wait_recv()
            fwd[k][i].start()
            copy = remote(to.at[i + 1], to.at[i + 1], twin_send.at[k, i + 1], twin_recv.at[k, i + 1], device_id=twin)
            copy.start()
            twins[k].append(copy)

    def share(k):
        to = lists_hbm.at[core, k]
        for copy in fwd[k]:
            copy.wait_recv()
        copy = remote(to.at[3], to.at[3], twin_send.at[k, 3], twin_recv.at[k, 3], device_id=twin)
        copy.start()
        twins[k].append(copy)

    def compute(k, between=None):
        if k >= 2:
            kept[k].wait()
        for copy in twins[k]:
            copy.wait_recv()
        pull = pltpu.make_async_copy(lists_hbm.at[:, k], lists, pull_sem.at[0])
        pull.start()
        acc[...] = jnp.zeros_like(acc)
        pull.wait()

        def gather(i, carry):
            cols = pl.ds(pl.multiple_of(i * step, step), step)
            left = lists[0, :, :, cols].reshape(ROWS, step)
            acc[0:ROWS, 0:hid] += nn(left, w_gate[cols, :])
            acc[0:ROWS, hid : 2 * hid] += nn(left, w_up[cols, :])
            acc[0:ROWS, 2 * hid : 3 * hid] += nt(lists[1, :, :, cols].reshape(ROWS, step), w_down[:, cols])
            return carry

        lax.fori_loop(0, width // step, gather, 0)
        part = all_part.at[k % 3]
        if k:
            parts[k - 1].wait_send()
        if k >= 3:
            for copy in far[k - 3] + near[k - 3]:
                copy.wait_send()
        for r in range(4):
            rows = slice(r * LIST, (r + 1) * LIST)
            tile = lists[0, r, :, width : width + LANES].astype(F32)
            mask = jnp.sum(jnp.where(iota(tile.shape, 1) == core, tile, 0.0), axis=1, keepdims=True)
            pre_gate = acc[rows, 0:hid]
            pre_up = acc[rows, hid : 2 * hid]
            scaled = acc[rows, 2 * hid : 3 * hid] * mask
            sig = jax.nn.sigmoid(pre_gate)
            act = pre_gate * sig
            slope = sig * (1.0 + pre_gate * (1.0 - sig))
            hidden = (act * pre_up).astype(BF).astype(F32) * mask
            piece = jnp.sum(hidden * scaled, axis=1, keepdims=True) * (1.0 / math.sqrt(width))
            acc[rows, 0:hid] = scaled * pre_up * slope
            acc[rows, hid : 2 * hid] = scaled * act
            acc[rows, 2 * hid : 3 * hid] = hidden
            wide = jnp.broadcast_to(piece, (LIST, LANES)).astype(BF)
            part[r, :, half:full] = wide
            twin_out[r, :, half:full] = wide
        if between is not None:
            between()
        packed[...] = acc[0:ROWS, 0 : 2 * hid].astype(BF)
        span = 512

        def rows_back(into, first):
            def one(i, carry):
                cols = pl.ds(pl.multiple_of(i * span, span), span)
                here = pl.ds(pl.multiple_of(first + i * span, span), span)
                total = nt(packed[:, 0:hid], w_gate[here, :]) + nt(packed[:, hid : 2 * hid], w_up[here, :])
                into[:, :, cols] = total.astype(BF).reshape(4, LIST, span)
                return carry

            lax.fori_loop(0, half // span, one, 0)

        rows_back(twin_out, other * half)
        if k:
            pl.semaphore_wait(part_free, 1)
        parts[k] = remote(twin_out, twin_in, part_send.at[k], part_recv.at[k], device_id=twin)
        parts[k].start()
        rows_back(part, core * half)
        turned[k] = jnp.transpose(acc[...]).astype(BF)

    def window(k):
        return (kept_cols, pl.ds(0, keep)) if k in OVER_Z else (pl.ds(0, full), pl.ds(0, full))

    def start_far(k):
        part = all_part.at[k % 3]
        far_in = all_far.at[k % 2]
        here, there = window(k)
        cut = 48 if k % 2 == 0 else 32
        low, up = pl.ds(0, cut), pl.ds(cut, LIST - cut)
        if k >= 2:
            pl.semaphore_wait(far_free.at[k % 2], 2)
        far[k] = [
            remote(part.at[3, low, here], far_in.at[0, low, there], far_send.at[k, 0], far_recv.at[k, 0], device_id=plus),
            remote(part.at[3, up, here], far_in.at[1, up, there], far_send.at[k, 1], far_recv.at[k, 1], device_id=minus),
        ]
        for copy in far[k]:
            copy.start()

    def merge(k):
        part = all_part.at[k % 3]
        parts[k].wait_recv()

        def add(r, carry):
            part[r] = (part[r].astype(F32) + twin_in[r].astype(F32)).astype(BF)
            return carry

        if k in OVER_Z:
            lax.fori_loop(0, 4, add, 0)
            if k != OVER_Z[0]:
                pl.semaphore_wait(z_free, 1)
            zs[k] = remote(part.at[:, :, sent_cols], z_in, z_send.at[k], z_recv.at[k], device_id=far_z)
            zs[k].start()
        else:
            add(3, 0)
            start_far(k)
            lax.fori_loop(0, 3, add, 0)
        if k < STEPS - 1:
            pl.semaphore_signal(part_free, 1, device_id=twin, device_id_type=MESH)

    def add_z(k):
        part = all_part.at[k % 3]
        zs[k].wait()

        def add(r, carry):
            part[r, :, kept_cols] = (part[r, :, kept_cols].astype(F32) + z_in[r].astype(F32)).astype(BF)
            return carry

        lax.fori_loop(0, 4, add, 0)
        if k != OVER_Z[-1]:
            pl.semaphore_signal(z_free, 1, device_id=far_z, device_id_type=MESH)
        start_far(k)

    def pass_on(k):
        part = all_part.at[k % 3]
        far_in, near_in = all_far.at[k % 2], all_near.at[k % 2]
        here, there = window(k)
        if k >= 2:
            pl.semaphore_wait(near_free.at[k % 2], 2)
        near[k] = [
            remote(part.at[2, :, here], near_in.at[0, :, there], near_send.at[k, 0], near_recv.at[k, 0], device_id=plus),
            remote(part.at[1, :, here], near_in.at[1, :, there], near_send.at[k, 1], near_recv.at[k, 1], device_id=minus),
        ]
        cut = 48 if k % 2 == 0 else 32
        for i, rel, rows, giver in ((0, 2, slice(0, cut), minus), (1, 1, slice(cut, LIST), plus)):
            far[k][i].wait_recv()
            part[rel, rows, here] = (part[rel, rows, here].astype(F32) + far_in[i, rows, there].astype(F32)).astype(BF)
            if k < STEPS - 2:
                pl.semaphore_signal(far_free.at[k % 2], 1, device_id=giver, device_id_type=MESH)
            near[k][i].start()

    def send_back(k):
        part = all_part.at[k % 3]
        near_in = all_near.at[k % 2]
        for copy in near[k]:
            copy.wait_recv()
        slot = k % 2
        if k >= 2:
            for copy in backs[k - 2]:
                copy.wait_send()
        if k in OVER_Z:
            back[slot] = jnp.zeros(back.shape[1:], BF)
            span = keep // 3
            for first in range(0, keep, span):
                there = pl.ds(pl.multiple_of(high * (full - keep) + first, LANES), span)
                total = tn(picks[k], part[0, :, there]) + tn(picks[k], near_in[0, :, first : first + span])
                total = total + tn(picks[k], near_in[1, :, first : first + span])
                if first == 0:
                    twice = (iota(total.shape, 1) < 2 * keep - full) & (high == 1)
                    total = jnp.where(twice, 0.0, total)
                back[slot, :, :, there] = total.astype(BF).reshape(BLOCKS, UNIT, span)
        for first in range(0, 0 if k in OVER_Z else full, 1024):
            cols = slice(first, min(first + 1024, full))
            total = tn(picks[k], part[0, :, cols]) + tn(picks[k], near_in[0, :, cols])
            total = total + tn(picks[k], near_in[1, :, cols])
            back[slot, :, :, cols] = total.astype(BF).reshape(BLOCKS, UNIT, cols.stop - cols.start)
        if k < STEPS - 2:
            for giver in (minus, plus):
                pl.semaphore_signal(near_free.at[k % 2], 1, device_id=giver, device_id_type=MESH)
        me = core * 16 + y * 4 + z
        backs[k] = []
        for dz in range(4):
            for dc in range(2):
                ay, az, ac = plane(k, dz, dc)
                src = back.at[slot, az * 2 + ac]
                index = (k * 4 + dz) * 2 + dc
                if k or dz or dc:
                    copy = remote(src, returned_hbm.at[me], back_send.at[index], back_recv.at[me], device_id=at(x, ay, az, ac))
                    copy.start()
                    backs[k].append(copy)
                else:
                    stay = pltpu.make_async_copy(src, returned_hbm.at[me], pull_sem.at[1])
                    stay.start()
                    stay.wait()

    flag_copies = []

    def tell():
        tile = jnp.maximum(lists[0, 0, 0:16, width : width + LANES], lists[0, 1, 0:16, width : width + LANES])
        tile = jnp.maximum(tile, lists[0, 2, 0:16, width : width + LANES])
        tile = jnp.maximum(tile, lists[0, 3, 0:16, width : width + LANES]).astype(F32)
        flag_out[...] = jnp.where(iota(tile.shape, 1) == 2, tile, 0.0).astype(BF)
        me = y * BLOCKS + mine
        for i, o in enumerate(offsets):
            if i:
                copy = remote(flag_out, flag_in.at[me], flag_send.at[i], flag_recv.at[me], device_id=at(x, *plane(*o)))
                copy.start()
                flag_copies.append(copy)
        flag_in[me] = flag_out[...]

    scale = 1.0 / math.sqrt(tokens * 8)
    span = 512
    blocks = width // span
    out_copies = []

    def stream(i, slot):
        cols = pl.ds(pl.multiple_of(i * span, span), span)
        made = []
        for k in range(STEPS):
            there = pl.ds(pl.multiple_of((slot * STEPS + k) * span, span), span)
            made.append(
                pltpu.make_async_copy(
                    lists_hbm.at[:, k, :, :, cols], lists.at[:, :, :, there], out_sem.at[slot * STEPS + k]
                )
            )
        return made

    def gradients(first, last):
        def one(i, carry):
            slot = lax.rem(i, 2)
            cols = pl.ds(pl.multiple_of(i * span, span), span)

            @pl.when(i + 1 < blocks)
            def _():
                for copy in stream(i + 1, 1 - slot):
                    copy.start()

            for copy in stream(i, slot):
                copy.wait()
            total = jnp.zeros((2 * hid, span), F32)
            down = jnp.zeros((hid, span), F32)
            for k in range(STEPS):
                there = pl.ds(pl.multiple_of((slot * STEPS + k) * span, span), span)
                total = total + nn(turned[k, 0 : 2 * hid, 0:ROWS], lists[0, :, :, there].reshape(ROWS, span))
                down = down + nn(turned[k, 2 * hid : 3 * hid, 0:ROWS], lists[1, :, :, there].reshape(ROWS, span))
            total = total * scale
            w_gate[cols, :] = jnp.transpose(total[0:hid]).astype(BF)
            w_up[cols, :] = jnp.transpose(total[hid : 2 * hid]).astype(BF)
            w_down[:, cols] = (down * scale).astype(BF)
            return carry

        if first == 0:
            for copy in stream(0, 0):
                copy.start()
        lax.fori_loop(first, last, one, 0)
        rows = pl.ds(first * span, (last - first) * span)
        n = 8 + len(out_copies)
        made = [
            pltpu.make_async_copy(w_gate.at[rows], grad_gate_hbm.at[0, rows], out_sem.at[n]),
            pltpu.make_async_copy(w_up.at[rows], grad_up_hbm.at[0, rows], out_sem.at[n + 1]),
            pltpu.make_async_copy(w_down.at[:, rows], grad_down_hbm.at[0, :, rows], out_sem.at[n + 2]),
        ]
        for copy in made:
            copy.start()
        out_copies.extend(made)

    units_out(0)
    for k in range(1, STEPS):
        units_over(k)
    take_in(0)
    units_out(1)
    take_in(1)
    units_out(2)
    forward(0)
    take_in(2)
    units_out(3)
    forward(1)
    share(0)
    take_in(3)
    for copy in weights:
        copy.wait()
    compute(0)
    merge(0)
    share(1)
    forward(2)
    compute(1)
    add_z(0)
    merge(1)
    share(2)
    forward(3)
    pass_on(0)
    add_z(1)
    compute(2)
    merge(2)
    share(3)
    send_back(0)
    pass_on(1)
    compute(3, lambda: pass_on(2))
    merge(3)
    send_back(1)
    tell()
    gradients(0, 2)
    send_back(2)
    pass_on(3)
    gradients(2, 7)
    send_back(3)
    gradients(7, 14)

    for dy, dz, dc in offsets[1:]:
        ay, az, ac = plane(dy, dz, dc)
        j = ac * 16 + ay * 4 + az
        pltpu.make_async_copy(back.at[0, 0], returned_hbm.at[j], back_recv.at[j]).wait()
        j = ay * BLOCKS + az * 2 + ac
        pltpu.make_async_copy(flag_out, flag_in.at[j], flag_recv.at[j]).wait()
    pull = pltpu.make_async_copy(returned_hbm, arrived.at[:, :, pl.ds(0, full)], pull_sem.at[0])
    pull.start()
    seen = jnp.max(flag_in[...].astype(F32).reshape(32 * 16, LANES), axis=0, keepdims=True)
    overflow[...] = jnp.broadcast_to(jnp.max(seen, axis=1, keepdims=True), overflow.shape)
    pull.wait()
    for h in range(2):
        for first in range(0, half, 512):
            found = arrived[h * 16 : (h + 1) * 16, :, first : first + 512].reshape(2 * SLOTS, 512)
            moe_grad[:, h * half + first : h * half + first + 512] = nn(token_map, found).astype(BF)
    found = arrived[0:16, :, half:full].reshape(2 * SLOTS, LANES)
    sums = nn(token_map, found)[:, 0:1] / gate
    gate_grad[...] = jnp.sum(jnp.where(diagonal, sums, 0.0), axis=0, keepdims=True).astype(BF)

    for copy in out_copies:
        copy.wait()
    for copy in unit_copies + flag_copies + [parts[STEPS - 1]]:
        copy.wait_send()
    for k in range(STEPS):
        done = fwd[k] + twins[k][1:] if k < 2 else own[k] + fwd[k] + twins[k]
        for copy in done:
            copy.wait_send()
    for k in range(STEPS - 3, STEPS):
        for copy in far[k] + near[k]:
            copy.wait_send()
    for copy in backs[STEPS - 2] + backs[STEPS - 1]:
        copy.wait_send()


def fast(moe_input, out_grad, expert_ids, gate_values, w_gate, w_up, w_down):
    tokens, width = moe_input.shape
    hid = w_gate.shape[2]
    full = width // 2 + LANES
    keep = (full // LANES + 1) // 2 * LANES
    vmem = pl.BlockSpec(memory_space=pltpu.VMEM)
    anywhere = pl.BlockSpec(memory_space=pl.ANY)
    dma = pltpu.SemaphoreType.DMA
    regular = pltpu.SemaphoreType.REGULAR
    return pl.pallas_call(
        kernel,
        out_shape=[
            jax.ShapeDtypeStruct((tokens, width), BF),
            jax.ShapeDtypeStruct((1, tokens), BF),
            jax.ShapeDtypeStruct((8, LANES), F32),
            jax.ShapeDtypeStruct(w_gate.shape, BF),
            jax.ShapeDtypeStruct(w_up.shape, BF),
            jax.ShapeDtypeStruct(w_down.shape, BF),
            jax.ShapeDtypeStruct((2, STEPS, 4, LIST, width + LANES), BF),
            jax.ShapeDtypeStruct((32, UNIT, full), BF),
        ],
        in_specs=[vmem] * 4 + [anywhere] * 3,
        out_specs=[vmem] * 3 + [anywhere] * 5,
        scratch_shapes=[
            pltpu.VMEM((width, hid), BF),
            pltpu.VMEM((width, hid), BF),
            pltpu.VMEM((hid, width), BF),
            pltpu.VMEM((4, 2, 2, UNIT, width), BF),
            pltpu.VMEM((STEPS - 1, 2, 2, UNIT, width), BF),
            pltpu.VMEM((STEPS * BLOCKS, UNIT, width), BF),
            pltpu.VMEM((2, LIST, width + LANES), BF),
            pltpu.VMEM((2, 4, LIST, width + LANES), BF),
            pltpu.VMEM((STEPS, LIST, SLOTS), BF),
            pltpu.VMEM((3, 4, LIST, full), BF),
            pltpu.VMEM((4, LIST, full), BF),
            pltpu.VMEM((4, LIST, full), BF),
            pltpu.VMEM((4, LIST, keep), BF),
            pltpu.VMEM((2, 2, LIST, full), BF),
            pltpu.VMEM((2, 2, LIST, full), BF),
            pltpu.VMEM((2, BLOCKS, UNIT, full), BF),
            pltpu.VMEM((PADDED, 3 * hid), F32),
            pltpu.VMEM((ROWS, 2 * hid), BF),
            pltpu.VMEM((STEPS, 3 * hid, PADDED), BF),
            pltpu.VMEM((16, LANES), BF),
            pltpu.VMEM((32, 16, LANES), BF),
            dma((3,)),
            dma((STEPS,)),
            dma((STEPS,)),
            dma((32,)),
            dma((32,)),
            dma((STEPS, 3)),
            dma((STEPS, 2)),
            dma((STEPS, 2)),
            dma((STEPS, 2)),
            dma((STEPS, 4)),
            dma((STEPS, 4)),
            dma((STEPS,)),
            dma((STEPS,)),
            dma((STEPS,)),
            dma((STEPS,)),
            dma((STEPS, 2)),
            dma((STEPS, 2)),
            dma((STEPS, 2)),
            dma((STEPS, 2)),
            regular,
            regular,
            pltpu.SemaphoreType.REGULAR((2,)),
            pltpu.SemaphoreType.REGULAR((2,)),
            dma((32,)),
            dma((32,)),
            dma((32,)),
            dma((32,)),
            dma((2,)),
            dma((17,)),
        ],
        compiler_params=pltpu.CompilerParams(
            collective_id=0, has_side_effects=True, vmem_limit_bytes=63 * 2**20
        ),
    )(moe_input, out_grad, expert_ids.reshape(1, tokens), gate_values.reshape(1, tokens), w_gate, w_up, w_down)


def silu_parts(value):
    sig = jax.nn.sigmoid(value)
    return (value * sig, sig * (1.0 + value * (1.0 - sig)))


def contract_rows(left, right):
    return lax.dot_general(
        left, right, (((0,), (0,)), ((), ())), preferred_element_type=jnp.float32
    )


def contract_cols(left, right):
    return lax.dot_general(
        left, right, (((1,), (1,)), ((), ())), preferred_element_type=jnp.float32
    )


def general(moe_input, out_grad, expert_ids, gate_values, w_gate, w_up, w_down):
    tok_rows = moe_input.shape[0]
    width = moe_input.shape[1]
    topw = expert_ids.shape[1]
    experts = lax.axis_size("ep")
    groups = lax.axis_size("fsdp")
    capacity = (3 * tok_rows * topw + experts - 1) // experts
    routes = tok_rows * topw
    flat_ids = expert_ids.reshape(routes)
    onehot = (flat_ids[:, None] == jnp.arange(experts, dtype=jnp.int32)[None, :]).astype(jnp.int32)
    earlier = jnp.cumsum(onehot, axis=0) - onehot
    slot_index = jnp.sum(earlier * onehot, axis=1)
    target = flat_ids * capacity + slot_index
    placing = (jnp.arange(experts * capacity, dtype=jnp.int32)[:, None] == target[None, :]).astype(
        jnp.bfloat16
    )
    route_input = jnp.repeat(moe_input, topw, axis=0)
    route_grad = jnp.repeat(out_grad, topw, axis=0)
    send_input = (
        jnp.dot(placing, route_input, preferred_element_type=jnp.float32)
        .astype(jnp.bfloat16)
        .reshape(experts, capacity, width)
    )
    send_grad = (
        jnp.dot(placing, route_grad, preferred_element_type=jnp.float32)
        .astype(jnp.bfloat16)
        .reshape(experts, capacity, width)
    )
    send_gate = jnp.sum(
        placing.astype(jnp.float32) * gate_values.reshape(1, routes).astype(jnp.float32), axis=1
    )
    send_gate = send_gate.astype(jnp.bfloat16).reshape(experts, capacity)
    recv_input, recv_grad, recv_gate = (
        lax.all_to_all(send_input, "ep", split_axis=0, concat_axis=0, tiled=True),
        lax.all_to_all(send_grad, "ep", split_axis=0, concat_axis=0, tiled=True),
        lax.all_to_all(send_gate, "ep", split_axis=0, concat_axis=0, tiled=True),
    )
    weight_gate = w_gate[0]
    weight_up = w_up[0]
    weight_down = w_down[0]
    expert_scale = 1.0 / math.sqrt(tok_rows * groups)
    gate_scale = 1.0 / math.sqrt(width)

    def gathered(own):
        copies = jnp.broadcast_to(own[None], (groups,) + own.shape)
        copies = lax.all_to_all(copies, "fsdp", split_axis=0, concat_axis=0, tiled=True)
        return copies.reshape((groups * own.shape[0],) + own.shape[1:])

    def summed(pieces):
        spread = lax.all_to_all(pieces, "fsdp", split_axis=0, concat_axis=0, tiled=True)
        spread = spread.reshape((groups, pieces.shape[0] // groups) + pieces.shape[1:])
        return jnp.sum(spread.astype(jnp.float32), axis=0)

    piece_input = gathered(recv_input)
    piece_grad = gathered(recv_grad)
    piece_gate = gathered(recv_gate)
    count = piece_input.shape[0] * piece_input.shape[1]
    rows_in = piece_input.reshape(count, width)
    rows_grad = piece_grad.reshape(count, width)
    gates = piece_gate.reshape(count, 1).astype(jnp.float32)
    pre_gate = jnp.dot(rows_in, weight_gate, preferred_element_type=jnp.float32)
    pre_up = jnp.dot(rows_in, weight_up, preferred_element_type=jnp.float32)
    act, slope = silu_parts(pre_gate)
    hidden = (act * pre_up).astype(jnp.bfloat16)
    raw = contract_cols(rows_grad, weight_down)
    scaled = gates * raw
    grad_pre_gate = (scaled * pre_up * slope).astype(jnp.bfloat16)
    grad_pre_up = (scaled * act).astype(jnp.bfloat16)
    gated_grad = (gates * rows_grad.astype(jnp.float32)).astype(jnp.bfloat16)
    acc_gate = contract_rows(rows_in, grad_pre_gate)
    acc_up = contract_rows(rows_in, grad_pre_up)
    acc_down = contract_rows(hidden, gated_grad)
    rows_back = contract_cols(grad_pre_gate, weight_gate) + contract_cols(grad_pre_up, weight_up)
    gate_back = jnp.sum(hidden.astype(jnp.float32) * raw, axis=1) * gate_scale
    part_rows = rows_back
    part_gate = gate_back
    acc_gate, acc_up, acc_down, part_rows, part_gate = (
        acc_gate,
        acc_up,
        acc_down,
        part_rows,
        part_gate,
    )
    grad_w_gate = (acc_gate * expert_scale).astype(jnp.bfloat16)[None]
    grad_w_up = (acc_up * expert_scale).astype(jnp.bfloat16)[None]
    grad_w_down = (acc_down * expert_scale).astype(jnp.bfloat16)[None]
    summed_rows = summed(part_rows.astype(jnp.bfloat16))
    summed_gate = summed(part_gate.astype(jnp.bfloat16))
    back_rows = summed_rows.astype(jnp.bfloat16).reshape(experts, capacity, width)
    back_gate = summed_gate.astype(jnp.bfloat16).reshape(experts, capacity)
    ret_rows, ret_gate = (
        lax.all_to_all(back_rows, "ep", split_axis=0, concat_axis=0, tiled=True),
        lax.all_to_all(back_gate, "ep", split_axis=0, concat_axis=0, tiled=True),
    )
    flat_rows = ret_rows.reshape(experts * capacity, width)
    route_back = contract_rows(placing, flat_rows)
    moe_grad = jnp.sum(route_back.reshape(tok_rows, topw, width), axis=1).astype(jnp.bfloat16)
    gate_back = jnp.sum(
        placing.astype(jnp.float32) * ret_gate.reshape(experts * capacity, 1).astype(jnp.float32),
        axis=0,
    )
    gate_grad = gate_back.reshape(tok_rows, topw).astype(jnp.bfloat16)
    return (moe_grad, gate_grad, grad_w_gate, grad_w_up, grad_w_down)


def body(*args):
    moe_grad, gate_row, overflow, grad_gate, grad_up, grad_down, _, _ = fast(*args)
    made = (moe_grad, gate_row.reshape(-1, 1), grad_gate, grad_up, grad_down)
    return lax.cond(overflow[0, 0] > 0.0, lambda: general(*args), lambda: made)


def solution(mesh):
    rows = P(("ep", "fsdp"), None)
    columns = P("ep", None, "fsdp")
    return jax.shard_map(
        body,
        mesh=mesh,
        in_specs=(rows, rows, rows, rows, columns, columns, P("ep", "fsdp", None)),
        out_specs=(rows, rows, columns, columns, P("ep", "fsdp", None)),
        check_vma=False,
    )
```
